32 devices in a mesh: groups: 2 (over y), gx: 4 (over z), gy: 4 (over x, core).
Axes of the slice: x: 2, y: 2, z: 4, core: 2. Of those that a mesh axis runs over, the one named last changes fastest.
Arguments:
- velocity0: float32 [6, 8, 4, 2048], P(None, ('groups', 'gx'), 'gy'), parts along dimension 1, may hold values from -6 to 6
- inv_mass: float32 [6, 8, 4, 2048], P(None, ('groups', 'gx'), 'gy'), parts along dimension 1, may hold values from 0.2 to 1
- jac_a: float32 [18, 8, 4, 32, 128], P(None, ('groups', 'gx'), 'gy'), parts along dimension 1, may hold values from -3 to 3
- jac_b: float32 [18, 8, 4, 32, 128], P(None, ('groups', 'gx'), 'gy'), parts along dimension 1, may hold values from -3 to 3
- precond: float32 [9, 8, 4, 32, 128], P(None, ('groups', 'gx'), 'gy'), parts along dimension 1, as said below
- bias: float32 [3, 8, 4, 32, 128], P(None, ('groups', 'gx'), 'gy'), parts along dimension 1, may hold values from -4 to 4
- friction: float32 [8, 4, 32, 128], P(('groups', 'gx'), 'gy'), parts along dimension 0, may hold values from 0.2 to 0.9
- impulse0: float32 [3, 8, 4, 32, 128], P(None, ('groups', 'gx'), 'gy'), parts along dimension 1, may hold values from -4 to 4
- body_a: int32 [8, 4, 32, 128], P(('groups', 'gx'), 'gy'), parts along dimension 0, may hold values from 0 to 2047
- body_b: int32 [8, 4, 32, 128], P(('groups', 'gx'), 'gy'), parts along dimension 0, may hold values from 0 to 3871, as said below
- active: int32 [8, 4, 32, 128], P(('groups', 'gx'), 'gy'), parts along dimension 0, may hold values 0 or 1
- sticking: int32 [8, 4, 32, 128], P(('groups', 'gx'), 'gy'), parts along dimension 0, may hold values 0 or 1
Outputs:
- impulses: float32 [3, 8, 4, 32, 128], P(None, ('groups', 'gx'), 'gy'), parts along dimension 1
- velocity: float32 [6, 8, 4, 2048], P(None, ('groups', 'gx'), 'gy'), parts along dimension 1
The draws below stay inside these ranges and needn't reach their ends.
There are 2 independent parts, one for each index of `groups`. The reference program is written for one: setup_inputs(seed, part) draws one part's arguments, and reference() takes and returns one part's arrays. A program takes and returns all parts, laid end to end along the dimension named above; each array names one. Nothing has to cross between parts.
Inputs may be any that keep to these rules, and one draw needn't show every extreme that they name: `body_b`: values under 2048 name a body of the contact's own device; a value 2048 + s * 256 + i names the body i of the neighbouring device in slot s's set facing back, with i under 256 // 8 for the corner slots 0, 2, 5, 7 and under 256 for the others; such a device always exists in the grid. `precond`: diagonal entries lie between 0.3 and 0.6, off-diagonal ones between -0.12 and 0.12.
All inputs are finite; a program needn't handle non-finite values. No bound on the sum of `active` or of `sticking` on one device may be relied on, other than what follows from the above.
Results may differ from the reference program's by a relative error of at most 0.0001.
Values sent between devices are 32-bit elements; how exact they have to be, the bound alone decides.
No kernel may reach another device: no remote copies, remote signals or barrier semaphores. Data moves between devices by JAX's collectives and lax.ppermute only.
A program may use at most 64 MiB of HBM per device.

```python
import math
import jax
import jax.numpy as jnp
import numpy as np
from jax import lax

ROWS = 3
DOF = 6
LANES = 128
NB = 2048
NBND = 256
CB = 32
ITERS = 3
GRID_X = 4
GRID_Y = 4


def draw_precond(key, part):
    key = jax.random.fold_in(key, 11)
    shape = (ROWS * ROWS, GRID_X, GRID_Y, CB, LANES)
    k_diag, k_off = jax.random.split(key)
    diag = jax.random.uniform(k_diag, shape, jnp.float32, 0.3, 0.6)
    off = jax.random.uniform(k_off, shape, jnp.float32, -0.12, 0.12)
    index = jax.lax.broadcasted_iota(jnp.int32, shape, 0)
    on_diag = index % (ROWS + 1) == 0
    return jnp.where(on_diag, diag, off)


def draw_body_b(key, part):
    key = jax.random.fold_in(key, 23)
    shape = (GRID_X, GRID_Y, CB, LANES)
    k_pick, k_local, k_far = jax.random.split(key, 3)
    pick = jax.random.randint(k_pick, shape, 0, 16)
    local = jax.random.randint(k_local, shape, 0, NB)
    raw_far = jax.random.randint(k_far, shape, 0, NBND)
    pos_x = jax.lax.broadcasted_iota(jnp.int32, shape, 0)
    pos_y = jax.lax.broadcasted_iota(jnp.int32, shape, 1)
    slot = jnp.minimum(pick, 7)
    is_corner = (slot == 0) | (slot == 2) | (slot == 5) | (slot == 7)
    far = jnp.where(is_corner, raw_far % (NBND // 8), raw_far)
    cell = slot + (slot >= 4).astype(jnp.int32)
    near_x = pos_x + cell // 3 - 1
    near_y = pos_y + cell % 3 - 1
    inside = (near_x >= 0) & (near_x < GRID_X) & (near_y >= 0) & (near_y < GRID_Y)
    use_far = (pick < 8) & inside
    coded = jnp.where(use_far, NB + slot * NBND + far, local)
    block = jax.lax.broadcasted_iota(jnp.int32, shape, 2)
    lane = jax.lax.broadcasted_iota(jnp.int32, shape, 3)
    last = (block == CB - 1) & (lane == LANES - 1)
    corner_ok = (pos_x < GRID_X - 1) & (pos_y < GRID_Y - 1)
    forced = jnp.where(corner_ok, NB + 7 * NBND + NBND // 8 - 1, NB - 1)
    return jnp.where(last, forced, coded).astype(jnp.int32)


def touch_ends(entries, stream_key, smallest, high):
    longest = entries.shape.index(max(entries.shape))
    spots = []
    for shift in (0, 1):
        where = [jax.random.randint(jax.random.fold_in(stream_key, axis), (), 0, length) for axis, length in enumerate(entries.shape)]
        where[longest] = (where[longest] + shift) % entries.shape[longest]
        spots.append(tuple(where))
    return entries.at[spots[0]].set(smallest).at[spots[1]].set(high)


def shard_levels(stream_key, shape, cuts, smallest, high):
    level, own = 1.0, jax.random.fold_in(stream_key, 6)
    for dim, shards_of in cuts:
        heights = jnp.exp(jax.random.uniform(jax.random.fold_in(own, dim), (shards_of,), jnp.float32, smallest / len(cuts), high / len(cuts)))
        level = level * jnp.repeat(heights, shape[dim] // shards_of).reshape([-1 if axis == dim else 1 for axis in range(len(shape))])
    return level


def bell_draw(rng, dims, spread, reach, cuts=(), dtype=jnp.bfloat16):
    values = jax.random.normal(rng, dims, jnp.float32) * spread
    if len(cuts) > 0:
        values = shard_levels(rng, dims, cuts, -0.22, 0.18) * values
    return jnp.clip(values, min=-reach, max=reach).astype(dtype)


def setup_inputs(seed: int = 0, part: int = 0) -> dict:
    key_list = jax.random.split(jax.random.key(seed), 13)
    part_keys = jax.random.split(jax.random.fold_in(key_list[12], part), 13)
    velocity0 = bell_draw(part_keys[0], (DOF, GRID_X, GRID_Y, NB), 1.0, 6.0, ((1, 4), (2, 4)), jnp.float32)
    inv_mass = jnp.clip(jnp.exp(math.log(1.0) - 1.609438 * jax.random.uniform(part_keys[1], (DOF, GRID_X, GRID_Y, NB), jnp.float32) ** shard_levels(part_keys[1], (DOF, GRID_X, GRID_Y, NB), ((1, 4), (2, 4)), -0.2, 0.2)), 0.2, 1.0)
    jac_a = bell_draw(part_keys[2], (ROWS * DOF, GRID_X, GRID_Y, CB, LANES), 0.4, 3.0, ((1, 4), (2, 4)), jnp.float32)
    jac_b = bell_draw(part_keys[3], (ROWS * DOF, GRID_X, GRID_Y, CB, LANES), 0.4, 3.0, ((1, 4), (2, 4)), jnp.float32)
    precond = draw_precond(jax.random.fold_in(jax.random.fold_in(key_list[12], part), 71), part)
    bias = bell_draw(part_keys[5], (ROWS, GRID_X, GRID_Y, CB, LANES), 0.5, 4.0, ((1, 4), (2, 4)), jnp.float32)
    friction = jnp.clip(jnp.exp(math.log(0.9) - 1.50407736 * jax.random.uniform(part_keys[6], (GRID_X, GRID_Y, CB, LANES), jnp.float32) ** shard_levels(part_keys[6], (GRID_X, GRID_Y, CB, LANES), ((0, 4), (1, 4)), -0.2, 0.2)), 0.2, 0.9)
    impulse0 = bell_draw(part_keys[7], (ROWS, GRID_X, GRID_Y, CB, LANES), 0.5, 4.0, ((1, 4), (2, 4)), jnp.float32)
    body_a = touch_ends(jax.random.randint(part_keys[8], (GRID_X, GRID_Y, CB, LANES), 0, NB), jax.random.fold_in(part_keys[8], 1), 0, NB - 1).astype(jnp.int32)
    body_b = draw_body_b(jax.random.fold_in(jax.random.fold_in(key_list[12], part), 71), part)
    active = touch_ends((jax.random.randint(part_keys[10], (GRID_X, GRID_Y, CB, LANES), 0, 4) < 3).astype(jnp.int32), jax.random.fold_in(part_keys[10], 1), 0, 1)
    sticking = touch_ends((jax.random.randint(part_keys[11], (GRID_X, GRID_Y, CB, LANES), 0, 2) < 1).astype(jnp.int32), jax.random.fold_in(part_keys[11], 1), 0, 1)
    return dict(velocity0=velocity0, inv_mass=inv_mass, jac_a=jac_a, jac_b=jac_b, precond=precond, bias=bias, friction=friction, impulse0=impulse0, body_a=body_a, body_b=body_b, active=active, sticking=sticking)


def project(raw, mu, stick, act):
    normal = jnp.maximum(raw[0], 0.0)
    bound = mu * (1.0 + 0.5 * stick) * normal + 0.1
    square = raw[1] * raw[1] + raw[2] * raw[2]
    scale = bound / jnp.sqrt(jnp.maximum(square, bound * bound))
    return act[None] * jnp.stack([normal, raw[1] * scale, raw[2] * scale])

def reference(velocity0, inv_mass, jac_a, jac_b, precond, bias, friction, impulse0, body_a, body_b, active, sticking):
    shape = body_a.shape
    corner = NBND // 8
    edge = NBND
    starts = np.array([0, corner, corner + edge, 2 * corner + edge, 2 * corner + 2 * edge, 2 * corner + 3 * edge, 3 * corner + 3 * edge, 3 * corner + 4 * edge])
    offsets = jnp.array(starts, jnp.int32)
    pos_x = jax.lax.broadcasted_iota(jnp.int32, shape, 0)
    pos_y = jax.lax.broadcasted_iota(jnp.int32, shape, 1)
    device = pos_x * GRID_Y + pos_y
    first = (device * NB + body_a).reshape(-1)
    far = body_b >= NB
    rel = jnp.maximum(body_b - NB, 0)
    slot = rel // NBND
    cells = jnp.array(np.array([0, 1, 2, 3, 5, 6, 7, 8]), jnp.int32)
    cell = cells[slot]
    near_dev = (pos_x + cell // 3 - 1) * GRID_Y + (pos_y + cell % 3 - 1)
    local = offsets[7 - slot] + rel % NBND
    second = jnp.where(far, near_dev * NB + local, device * NB + body_b).reshape(-1)
    j_a = jac_a.reshape(ROWS, DOF, -1)
    j_b = jac_b.reshape(ROWS, DOF, -1)
    w_mat = precond.reshape(ROWS, ROWS, -1)
    bias_flat = bias.reshape(ROWS, -1)
    mu = friction.reshape(-1)
    stick = sticking.reshape(-1).astype(jnp.float32)
    act = active.reshape(-1).astype(jnp.float32)
    start = velocity0.reshape(DOF, -1)
    minv = inv_mass.reshape(DOF, -1)

    def velocities(lam):
        force_a = lax.optimization_barrier(jnp.sum(j_a * lam[:, None], axis=0))
        force_b = lax.optimization_barrier(jnp.sum(j_b * lam[:, None], axis=0))
        total = jnp.zeros(start.shape, jnp.float32).at[:, first].add(force_a).at[:, second].add(force_b)
        return start + minv * total
    lam = act[None] * impulse0.reshape(ROWS, -1)
    for step in range(ITERS):
        vel = velocities(lam)
        rel_vel = lax.optimization_barrier(jnp.sum(j_a * vel[:, first][None], axis=1)) + lax.optimization_barrier(jnp.sum(j_b * vel[:, second][None], axis=1))
        target = rel_vel + bias_flat
        change = lax.optimization_barrier(jnp.sum(w_mat * target[None], axis=1))
        lam = project(lam - change, mu, stick, act)
    vel = velocities(lam)
    return (lam.reshape(impulse0.shape), vel.reshape(velocity0.shape))
```

```python
import jax
import jax.numpy as jnp
import numpy as np
from jax import lax
from jax.experimental import pallas as pl
from jax.experimental.pallas import tpu as pltpu
from jax.sharding import PartitionSpec as P

ROWS = 3
DOF = 6
ITERS = 3
LANES = 128
NB = 2048
NBND = 256
CORNER = NBND // 8
OWN_TILES = NB // LANES
EDGE_TILES = 2
HALO_TILES = 9
CORNER_TILE = OWN_TILES - 1
HALO_CORNER = HALO_TILES - 1
SET_START = (0, 32, 288, 320, 576, 832, 864, 1120)
TABLE_START = (1920, 0, 1952, 256, 512, 1984, 768, 2016)
INTERIOR_START = 1152
INTERIOR_TABLE = 1024
EDGE_SLOTS = (1, 3, 4, 6)
CORNER_SLOTS = (0, 2, 5, 7)


def table_index(body):
    steps = []
    for slot in range(8):
        steps.append((SET_START[slot], TABLE_START[slot] - SET_START[slot]))
    steps.append((INTERIOR_START, INTERIOR_TABLE - INTERIOR_START))
    for slot in range(8):
        steps.append((NB + slot * NBND, TABLE_START[slot] - slot * NBND))
    shift = jnp.full(body.shape, steps[0][1], jnp.int32)
    for start, delta in steps[1:]:
        shift = jnp.where(body >= start, delta, shift)
    return body + shift


def lane_iota():
    return lax.broadcasted_iota(jnp.int32, (8, LANES), 1)


def to_tables(ref):
    zero = jnp.zeros((2, LANES), jnp.float32)
    blocks = [
        jnp.concatenate([ref[pl.ds(k, DOF, stride=OWN_TILES), :], zero], axis=0)
        for k in range(OWN_TILES)
    ]
    lane = lane_iota()
    tiles = []
    for slot in EDGE_SLOTS:
        first, off = divmod(SET_START[slot], LANES)
        rolled = [pltpu.roll(blocks[first + j], LANES - off, 1) for j in range(3)]
        for j in range(2):
            tiles.append(jnp.where(lane < LANES - off, rolled[j], rolled[j + 1]))
    tiles += blocks[INTERIOR_START // LANES :]
    corner = jnp.zeros((8, LANES), jnp.float32)
    for place, slot in enumerate(CORNER_SLOTS):
        block = blocks[SET_START[slot] // LANES]
        corner = jnp.where(lane // CORNER == place, block, corner)
    tiles.append(corner)
    return tiles


def from_tables(tiles, out_ref):
    lane = lane_iota()
    blocks = [jnp.zeros((8, LANES), jnp.float32) for _ in range(INTERIOR_START // LANES)]
    for e, slot in enumerate(EDGE_SLOTS):
        first, off = divmod(SET_START[slot], LANES)
        rolled = [pltpu.roll(tiles[2 * e + j], off, 1) for j in range(2)]
        blocks[first] = jnp.where(lane >= off, rolled[0], blocks[first])
        blocks[first + 1] = jnp.where(lane >= off, rolled[1], rolled[0])
        blocks[first + 2] = jnp.where(lane < off, rolled[1], blocks[first + 2])
    for place, slot in enumerate(CORNER_SLOTS):
        k = SET_START[slot] // LANES
        blocks[k] = jnp.where(lane // CORNER == place, tiles[CORNER_TILE], blocks[k])
    blocks += tiles[8:CORNER_TILE]
    for k in range(OWN_TILES):
        out_ref[pl.ds(k, DOF, stride=OWN_TILES), :] = blocks[k][:DOF]


def row_of(ref, r):
    return ref[pl.ds(r, 1), :]


def build_onehot(index_ref, onehot_ref):
    rows = index_ref.shape[0]
    base = lax.broadcasted_iota(jnp.int32, (NBND, LANES), 0)
    for r in range(rows):
        q = row_of(index_ref, r) & (NBND - 1)
        hit = (base == q).astype(jnp.float32).astype(jnp.bfloat16)
        onehot_ref[:, r * LANES : (r + 1) * LANES] = hit


def forces(lam, jac_ref, force_ref):
    rows = lam[0].shape[0]
    for d in range(DOF):
        f = jac_ref[d] * lam[0]
        f = f + jac_ref[DOF + d] * lam[1]
        f = f + jac_ref[2 * DOF + d] * lam[2]
        force_ref[d * rows : (d + 1) * rows, :] = f
    for d in range(DOF, 8):
        force_ref[d * rows : (d + 1) * rows, :] = jnp.zeros_like(f)


def spread(force_ref, index_ref, left_ref, heads):
    rows = index_ref.shape[0]
    for r in range(rows):
        f = force_ref[pl.ds(r, 8, stride=rows), :]
        hi = f.astype(jnp.bfloat16).astype(jnp.float32)
        lo = f - hi
        both = jnp.concatenate([hi, lo], axis=0)
        head = jnp.broadcast_to(row_of(index_ref, r) >> 8, (16, LANES))
        for k, h in enumerate(heads):
            left_ref[16 * k : 16 * (k + 1), r * LANES : (r + 1) * LANES] = jnp.where(
                head == h, both, 0.0
            ).astype(jnp.bfloat16)


OWN_HEADS = tuple(range(8))
ALL_HEADS = OWN_HEADS + (8, 9, 10, 11, 15)


def scatter(lam, jac_a, jac_b, id_a, id_b, hot_a, hot_b, force, left_a, left_b):
    contract = (((1,), (1,)), ((), ()))
    forces(lam, jac_a, force)
    spread(force, id_a, left_a, OWN_HEADS)
    sum_a = lax.dot_general(left_a[...], hot_a[...], contract, preferred_element_type=jnp.float32)
    forces(lam, jac_b, force)
    spread(force, id_b, left_b, ALL_HEADS)
    sum_b = lax.dot_general(left_b[...], hot_b[...], contract, preferred_element_type=jnp.float32)

    def tile(s, k, j):
        lanes = slice(j * LANES, (j + 1) * LANES)
        return s[16 * k : 16 * k + 8, lanes] + s[16 * k + 8 : 16 * k + 16, lanes]

    own = [tile(sum_a, t // 2, t % 2) + tile(sum_b, t // 2, t % 2) for t in range(OWN_TILES)]
    halo = [tile(sum_b, 8 + t // 2, t % 2) for t in range(8)] + [tile(sum_b, 12, 1)]
    return own, halo


def put_x(even, planes, a_ref, b_ref):
    high = lane_iota() >= 2 * CORNER
    for p, tiles in enumerate(planes):
        up = (tiles[6], tiles[7], jnp.where(high, tiles[-1], 0.0))
        down = (tiles[0], tiles[1], jnp.where(high, 0.0, tiles[-1]))
        for k in range(3):
            a_ref[p, k] = jnp.where(even, up[k], down[k])
            b_ref[p, k] = jnp.where(even, down[k], up[k])


def is_even():
    return lax.rem(lax.axis_index("gy"), 2) == 0


def corners_in(y_low, y_high, p):
    lane = lane_iota()
    odd = (lane & CORNER) != 0
    return jnp.where(odd, pltpu.roll(y_high(p, 2), 96, 1), pltpu.roll(y_low(p, 2), 32, 1))


class Received:
    def __init__(self, even, a_ref, b_ref, e_ref, o_ref):
        def pick(first, second):
            return lambda p, k: jnp.where(even, first[p, k], second[p, k])

        self.x_low, self.x_high = pick(a_ref, b_ref), pick(b_ref, a_ref)
        if e_ref is not None:
            self.y_high, self.y_low = pick(e_ref, o_ref), pick(o_ref, e_ref)

    def plane(self, p):
        tiles = []
        for side in (self.x_low, self.y_low, self.y_high, self.x_high):
            tiles += [side(p, 0), side(p, 1)]
        return tiles + [corners_in(self.y_low, self.y_high, p)]


def add_own(own, came):
    out = [own[t] + came[t] for t in range(8)]
    out += [own[t] for t in range(8, CORNER_TILE)]
    return out + [own[CORNER_TILE] + came[HALO_CORNER]]


def first_kernel(*refs):
    sources, kept, outs = refs[:12], refs[12:20], refs[20:30]
    body_a, body_b, start, minv, force, left_a, left_b, sems = refs[30:]
    id_a, id_b, hot_a, hot_b, own, halo, v_own, m_own, xa, xb = outs
    jac_a, jac_b, precond, bias, mu, stick, act, lam0 = kept
    goals = (body_a, body_b, act, lam0, jac_a, jac_b, start, minv, precond, bias, mu, stick)
    copies = [pltpu.make_async_copy(s, g, sems.at[k]) for k, (s, g) in enumerate(zip(sources, goals))]
    for copy in copies:
        copy.start()
    even = is_even()
    copies[0].wait()
    id_a[...] = table_index(body_a[...])
    build_onehot(id_a, hot_a)
    copies[1].wait()
    id_b[...] = table_index(body_b[...])
    build_onehot(id_b, hot_b)
    for copy in copies[2:6]:
        copy.wait()
    active = act[...].astype(jnp.float32)
    lam = [active * lam0[k] for k in range(ROWS)]
    sums, sums_halo = scatter(lam, jac_a, jac_b, id_a, id_b, hot_a, hot_b, force, left_a, left_b)
    for copy in copies[6:8]:
        copy.wait()
    v, m = to_tables(start), to_tables(minv)
    for t in range(OWN_TILES):
        own[t], v_own[t], m_own[t] = sums[t], v[t], m[t]
    for t in range(HALO_TILES):
        halo[t] = sums_halo[t]
    put_x(even, [sums, sums_halo, v, m], xa, xb)
    for copy in copies[8:]:
        copy.wait()


def turn_kernel(planes, ra, rb, *refs):
    sources, (e_ref, o_ref) = refs[:-2], refs[-2:]
    even = is_even()
    came = Received(even, ra, rb, None, None)
    lane = lane_iota()
    for p in range(planes):
        corner = jnp.where(lane < 2 * CORNER, came.x_high(p, 2), came.x_low(p, 2))
        for k in range(2):
            minus, plus = sources[p][2 + k], sources[p][4 + k]
            e_ref[p, k] = jnp.where(even, plus, minus)
            o_ref[p, k] = jnp.where(even, minus, plus)
        e_ref[p, 2] = corner
        o_ref[p, 2] = corner


TILE_CODES = tuple((t, t) for t in range(24)) + ((31, 24),)


def gather(table, index, codes):
    lane = index & (LANES - 1)
    code = index >> 7
    values = [jnp.zeros(index.shape, jnp.float32) for _ in range(DOF)]
    for c, t in codes:
        mask = code == c
        for d in range(DOF):
            row = jnp.broadcast_to(table[t, d : d + 1, :], index.shape)
            got = jnp.take_along_axis(row, lane, axis=1, mode="promise_in_bounds")
            values[d] = jnp.where(mask, got, values[d])
    return values


def relative(jac, values):
    out = []
    for k in range(ROWS):
        u = jac[k * DOF] * values[0]
        for d in range(1, DOF):
            u = u + jac[k * DOF + d] * values[d]
        out.append(u)
    return out


def middle_kernel(
    first, jac_a, jac_b, precond, bias, mu, stick, act, lam_in,
    id_a, id_b, hot_a, hot_b, own, halo, v_own, m_own, *refs,
):
    if first:
        ra, rb, qe, qo, lam_out, own_out, halo_out, xa, xb, v_halo, m_halo = refs[:11]
    else:
        v_halo, m_halo, ra, rb, qe, qo, lam_out, own_out, halo_out, xa, xb = refs[:11]
    table, force, left_a, left_b = refs[11:]
    even = is_even()
    came = Received(even, ra, rb, qe, qo)
    if first:
        for ref, p in ((v_halo, 2), (m_halo, 3)):
            for t, value in enumerate(came.plane(p)):
                ref[t] = value
    total = add_own(own, came.plane(1))
    total_halo = [a + b for a, b in zip([halo[t] for t in range(HALO_TILES)], came.plane(0))]
    for t in range(OWN_TILES):
        table[t] = v_own[t] + m_own[t] * total[t]
    for t in range(HALO_TILES):
        table[OWN_TILES + t] = v_halo[t] + m_halo[t] * total_halo[t]
    u_a = relative(jac_a, gather(table, id_a[...], TILE_CODES[:OWN_TILES]))
    u_b = relative(jac_b, gather(table, id_b[...], TILE_CODES))
    target = [u_a[k] + u_b[k] + bias[k] for k in range(ROWS)]
    active = act[...].astype(jnp.float32)
    if first:
        lam = [active * lam_in[k] for k in range(ROWS)]
    else:
        lam = [lam_in[k] for k in range(ROWS)]
    raw = []
    for k in range(ROWS):
        w = precond[k * ROWS] * target[0]
        for j in range(1, ROWS):
            w = w + precond[k * ROWS + j] * target[j]
        raw.append(lam[k] - w)
    normal = jnp.maximum(raw[0], 0.0)
    bound = mu[...] * (1.0 + 0.5 * stick[...].astype(jnp.float32)) * normal + 0.1
    square = raw[1] * raw[1] + raw[2] * raw[2]
    scale = bound / jnp.sqrt(jnp.maximum(square, bound * bound))
    lam = [active * normal, active * (raw[1] * scale), active * (raw[2] * scale)]
    for k in range(ROWS):
        lam_out[k] = lam[k]
    sums, sums_halo = scatter(lam, jac_a, jac_b, id_a, id_b, hot_a, hot_b, force, left_a, left_b)
    for t in range(OWN_TILES):
        own_out[t] = sums[t]
    for t in range(HALO_TILES):
        halo_out[t] = sums_halo[t]
    put_x(even, [sums, sums_halo], xa, xb)


def last_kernel(own, v_own, m_own, ra, rb, qe, qo, out):
    came = Received(is_even(), ra, rb, qe, qo)
    total = add_own(own, came.plane(1))
    from_tables([v_own[t] + m_own[t] * total[t] for t in range(OWN_TILES)], out)


def exchange_pairs(nx, ny):
    up = []
    for x in range(nx):
        for y in range(ny):
            to = x + 1 if y % 2 == 0 else x - 1
            goal = (to, y) if 0 <= to < nx else (x, y ^ 1)
            up.append((x * ny + y, goal[0] * ny + goal[1]))
    down = [(b, a) for a, b in up]
    near = [(y, y ^ 1) for y in range(ny)]
    far = [(y, (((y + 1) ^ 1) - 1) % ny) for y in range(ny)]
    return up, down, near, far


def on_device(
    velocity0, inv_mass, jac_a, jac_b, precond, bias, friction, impulse0, body_a, body_b, active, sticking
):
    nx, ny = lax.axis_size("gx"), lax.axis_size("gy")
    up, down, near, far = exchange_pairs(nx, ny)
    rows, lanes = body_a.shape[-2:]
    flat = lambda a: a.reshape(-1, rows, lanes)
    plain = lambda a: a.reshape(rows, lanes)
    jac_a, jac_b, precond, bias, impulse0 = map(flat, (jac_a, jac_b, precond, bias, impulse0))
    friction, body_a, body_b, active, sticking = map(plain, (friction, body_a, body_b, active, sticking))
    start, minv = (a.reshape(-1, lanes) for a in (velocity0, inv_mass))
    contacts = rows * lanes
    f32, i32, bf16 = jnp.float32, jnp.int32, jnp.bfloat16
    arr = jax.ShapeDtypeStruct
    vmem = pl.BlockSpec(memory_space=pltpu.VMEM)
    own_t, halo_t = arr((OWN_TILES, 8, lanes), f32), arr((HALO_TILES, 8, lanes), f32)
    lam_t = arr((ROWS, rows, lanes), f32)
    ids_t, hot_t = arr((rows, lanes), i32), arr((NBND, contacts), bf16)
    message = lambda p: arr((p, 3, 8, lanes), f32)
    work = [
        pltpu.VMEM((8 * rows, lanes), f32),
        pltpu.VMEM((16 * len(OWN_HEADS), contacts), bf16),
        pltpu.VMEM((16 * len(ALL_HEADS), contacts), bf16),
    ]
    table = [pltpu.VMEM((OWN_TILES + HALO_TILES, 8, lanes), f32)]

    def call(kernel, outs, scratch, name, *operands, space=pltpu.VMEM):
        return pl.pallas_call(
            kernel,
            out_shape=outs,
            in_specs=[pl.BlockSpec(memory_space=space)] * len(operands),
            out_specs=jax.tree.map(lambda _: vmem, outs),
            scratch_shapes=scratch,
            compiler_params=pltpu.CompilerParams(vmem_limit_bytes=32 * 1024 * 1024),
            name=name,
        )(*operands)

    def exchange(xa, xb, sources):
        planes = xa.shape[0]
        ra = lax.ppermute(xa, ("gx", "gy"), up)
        rb = lax.ppermute(xb, ("gx", "gy"), down)
        ye, yo = call(
            lambda *refs: turn_kernel(planes, *refs), (message(planes), message(planes)), [], "turn", ra, rb, *sources
        )
        return ra, rb, lax.ppermute(ye, "gy", near), lax.ppermute(yo, "gy", far)

    sources = (body_a, body_b, active, impulse0, jac_a, jac_b, start, minv, precond, bias, friction, sticking)
    like = lambda a: arr(a.shape, a.dtype)
    kept = (jac_a, jac_b, precond, bias, friction, sticking, active, impulse0)
    made = call(
        first_kernel,
        (*map(like, kept), ids_t, ids_t, hot_t, hot_t, own_t, halo_t, own_t, own_t, message(4), message(4)),
        [pltpu.VMEM(a.shape, a.dtype) for a in (body_a, body_b, start, minv)]
        + work
        + [pltpu.SemaphoreType.DMA((len(sources),))],
        "first",
        *sources,
        space=pltpu.HBM,
    )
    fixed, lam = made[:7], made[7]
    id_a, id_b, hot_a, hot_b, own, halo, v_own, m_own, xa, xb = made[8:]
    for step in range(ITERS):
        first = step == 0
        sources = (own, halo, v_own, m_own) if first else (own, halo)
        received = exchange(xa, xb, sources)
        ins = (*fixed, lam, id_a, id_b, hot_a, hot_b, own, halo, v_own, m_own)
        outs = (lam_t, own_t, halo_t, message(2), message(2))
        kernel = lambda *refs, first=first: middle_kernel(first, *refs)
        if first:
            lam, own, halo, xa, xb, v_halo, m_halo = call(
                kernel, outs + (halo_t, halo_t), table + work, "middle0", *ins, *received
            )
        else:
            lam, own, halo, xa, xb = call(
                kernel, outs, table + work, "middle", *ins, v_halo, m_halo, *received
            )
    received = exchange(xa, xb, (own, halo))
    out = call(last_kernel, arr(start.shape, f32), [], "last", own, v_own, m_own, *received)
    return lam.reshape(ROWS, 1, 1, rows, lanes), out.reshape(velocity0.shape)


def solution(mesh):
    whole = ("groups", "gx")
    body = P(None, whole, "gy", None)
    many = P(None, whole, "gy", None, None)
    one = P(whole, "gy", None, None)
    return jax.shard_map(
        on_device,
        mesh=mesh,
        in_specs=(body, body, many, many, many, many, one, many, one, one, one, one),
        out_specs=(many, body),
        check_vma=False,
    )
```

```python
import jax
import jax.numpy as jnp
import numpy as np
from jax import lax
from jax.experimental import pallas as pl
from jax.experimental.pallas import tpu as pltpu
from jax.sharding import PartitionSpec as P

ROWS = 3
DOF = 6
ITERS = 3
LANES = 128
NB = 2048
NBND = 256
CORNER = NBND // 8
OWN_TILES = NB // LANES
EDGE_TILES = 2
HALO_TILES = 9
CORNER_TILE = OWN_TILES - 1
HALO_CORNER = HALO_TILES - 1
SET_START = (0, 32, 288, 320, 576, 832, 864, 1120)
TABLE_START = (1920, 0, 1952, 256, 512, 1984, 768, 2016)
INTERIOR_START = 1152
INTERIOR_TABLE = 1024
EDGE_SLOTS = (1, 3, 4, 6)
CORNER_SLOTS = (0, 2, 5, 7)


def table_index(body):
    steps = []
    for slot in range(8):
        steps.append((SET_START[slot], TABLE_START[slot] - SET_START[slot]))
    steps.append((INTERIOR_START, INTERIOR_TABLE - INTERIOR_START))
    for slot in range(8):
        steps.append((NB + slot * NBND, TABLE_START[slot] - slot * NBND))
    shift = jnp.full(body.shape, steps[0][1], jnp.int32)
    for start, delta in steps[1:]:
        shift = jnp.where(body >= start, delta, shift)
    return body + shift


def lane_iota():
    return lax.broadcasted_iota(jnp.int32, (8, LANES), 1)


def to_tables(ref):
    zero = jnp.zeros((2, LANES), jnp.float32)
    blocks = [
        jnp.concatenate([ref[pl.ds(k, DOF, stride=OWN_TILES), :], zero], axis=0)
        for k in range(OWN_TILES)
    ]
    lane = lane_iota()
    tiles = []
    for slot in EDGE_SLOTS:
        first, off = divmod(SET_START[slot], LANES)
        rolled = [pltpu.roll(blocks[first + j], LANES - off, 1) for j in range(3)]
        for j in range(2):
            tiles.append(jnp.where(lane < LANES - off, rolled[j], rolled[j + 1]))
    tiles += blocks[INTERIOR_START // LANES :]
    corner = jnp.zeros((8, LANES), jnp.float32)
    for place, slot in enumerate(CORNER_SLOTS):
        block = blocks[SET_START[slot] // LANES]
        corner = jnp.where(lane // CORNER == place, block, corner)
    tiles.append(corner)
    return tiles


def from_tables(tiles, out_ref):
    lane = lane_iota()
    blocks = [jnp.zeros((8, LANES), jnp.float32) for _ in range(INTERIOR_START // LANES)]
    for e, slot in enumerate(EDGE_SLOTS):
        first, off = divmod(SET_START[slot], LANES)
        rolled = [pltpu.roll(tiles[2 * e + j], off, 1) for j in range(2)]
        blocks[first] = jnp.where(lane >= off, rolled[0], blocks[first])
        blocks[first + 1] = jnp.where(lane >= off, rolled[1], rolled[0])
        blocks[first + 2] = jnp.where(lane < off, rolled[1], blocks[first + 2])
    for place, slot in enumerate(CORNER_SLOTS):
        k = SET_START[slot] // LANES
        blocks[k] = jnp.where(lane // CORNER == place, tiles[CORNER_TILE], blocks[k])
    blocks += tiles[8:CORNER_TILE]
    for k in range(OWN_TILES):
        out_ref[pl.ds(k, DOF, stride=OWN_TILES), :] = blocks[k][:DOF]


def row_of(ref, r):
    return ref[pl.ds(r, 1), :]


def build_onehot(index_ref, onehot_ref):
    rows = index_ref.shape[0]
    base = lax.broadcasted_iota(jnp.int32, (NBND, LANES), 0)
    for r in range(rows):
        q = row_of(index_ref, r) & (NBND - 1)
        hit = (base == q).astype(jnp.float32).astype(jnp.bfloat16)
        onehot_ref[:, r * LANES : (r + 1) * LANES] = hit


def forces(lam, jac_ref, force_ref):
    rows = lam[0].shape[0]
    for d in range(DOF):
        f = jac_ref[d] * lam[0]
        f = f + jac_ref[DOF + d] * lam[1]
        f = f + jac_ref[2 * DOF + d] * lam[2]
        force_ref[d * rows : (d + 1) * rows, :] = f
    for d in range(DOF, 8):
        force_ref[d * rows : (d + 1) * rows, :] = jnp.zeros_like(f)


def spread(force_ref, index_ref, left_ref, heads):
    rows = index_ref.shape[0]
    for r in range(rows):
        f = force_ref[pl.ds(r, 8, stride=rows), :]
        hi = f.astype(jnp.bfloat16).astype(jnp.float32)
        lo = f - hi
        both = jnp.concatenate([hi, lo], axis=0)
        head = jnp.broadcast_to(row_of(index_ref, r) >> 8, (16, LANES))
        for k, h in enumerate(heads):
            left_ref[16 * k : 16 * (k + 1), r * LANES : (r + 1) * LANES] = jnp.where(
                head == h, both, 0.0
            ).astype(jnp.bfloat16)


OWN_HEADS = tuple(range(8))
ALL_HEADS = OWN_HEADS + (8, 9, 10, 11, 15)


def scatter(lam, jac_a, jac_b, id_a, id_b, hot_a, hot_b, force, left_a, left_b):
    contract = (((1,), (1,)), ((), ()))
    forces(lam, jac_a, force)
    spread(force, id_a, left_a, OWN_HEADS)
    sum_a = lax.dot_general(left_a[...], hot_a[...], contract, preferred_element_type=jnp.float32)
    forces(lam, jac_b, force)
    spread(force, id_b, left_b, ALL_HEADS)
    sum_b = lax.dot_general(left_b[...], hot_b[...], contract, preferred_element_type=jnp.float32)

    def tile(s, k, j):
        lanes = slice(j * LANES, (j + 1) * LANES)
        return s[16 * k : 16 * k + 8, lanes] + s[16 * k + 8 : 16 * k + 16, lanes]

    own = [tile(sum_a, t // 2, t % 2) + tile(sum_b, t // 2, t % 2) for t in range(OWN_TILES)]
    halo = [tile(sum_b, 8 + t // 2, t % 2) for t in range(8)] + [tile(sum_b, 12, 1)]
    return own, halo


def put_x(even, planes, a_ref, b_ref):
    high = lane_iota() >= 2 * CORNER
    for p, tiles in enumerate(planes):
        up = (tiles[6], tiles[7], jnp.where(high, tiles[-1], 0.0))
        down = (tiles[0], tiles[1], jnp.where(high, 0.0, tiles[-1]))
        for k in range(3):
            a_ref[p, k] = jnp.where(even, up[k], down[k])
            b_ref[p, k] = jnp.where(even, down[k], up[k])


def is_even():
    return lax.rem(lax.axis_index("gy"), 2) == 0


def corners_in(y_low, y_high, p):
    lane = lane_iota()
    odd = (lane & CORNER) != 0
    return jnp.where(odd, pltpu.roll(y_high(p, 2), 96, 1), pltpu.roll(y_low(p, 2), 32, 1))


class Received:
    def __init__(self, even, a_ref, b_ref, e_ref, o_ref):
        def pick(first, second):
            return lambda p, k: jnp.where(even, first[p, k], second[p, k])

        self.x_low, self.x_high = pick(a_ref, b_ref), pick(b_ref, a_ref)
        if e_ref is not None:
            self.y_high, self.y_low = pick(e_ref, o_ref), pick(o_ref, e_ref)

    def plane(self, p):
        tiles = []
        for side in (self.x_low, self.y_low, self.y_high, self.x_high):
            tiles += [side(p, 0), side(p, 1)]
        return tiles + [corners_in(self.y_low, self.y_high, p)]


def add_own(own, came):
    out = [own[t] + came[t] for t in range(8)]
    out += [own[t] for t in range(8, CORNER_TILE)]
    return out + [own[CORNER_TILE] + came[HALO_CORNER]]


def first_kernel(*refs):
    sources, kept, outs = refs[:12], refs[12:20], refs[20:30]
    body_a, body_b, start, minv, force, left_a, left_b, sems = refs[30:]
    id_a, id_b, hot_a, hot_b, own, halo, v_own, m_own, xa, xb = outs
    jac_a, jac_b, precond, bias, mu, stick, act, lam0 = kept
    goals = (body_a, body_b, act, lam0, jac_a, jac_b, start, minv, precond, bias, mu, stick)
    copies = [pltpu.make_async_copy(s, g, sems.at[k]) for k, (s, g) in enumerate(zip(sources, goals))]
    for copy in copies:
        copy.start()
    even = is_even()
    copies[0].wait()
    id_a[...] = table_index(body_a[...])
    build_onehot(id_a, hot_a)
    copies[1].wait()
    id_b[...] = table_index(body_b[...])
    build_onehot(id_b, hot_b)
    for copy in copies[2:6]:
        copy.wait()
    active = act[...].astype(jnp.float32)
    lam = [active * lam0[k] for k in range(ROWS)]
    sums, sums_halo = scatter(lam, jac_a, jac_b, id_a, id_b, hot_a, hot_b, force, left_a, left_b)
    for copy in copies[6:8]:
        copy.wait()
    v, m = to_tables(start), to_tables(minv)
    for t in range(OWN_TILES):
        own[t], v_own[t], m_own[t] = sums[t], v[t], m[t]
    for t in range(HALO_TILES):
        halo[t] = sums_halo[t]
    put_x(even, [sums, sums_halo, v, m], xa, xb)
    for copy in copies[8:]:
        copy.wait()


def turn_kernel(planes, ra, rb, *refs):
    sources, (e_ref, o_ref) = refs[:-2], refs[-2:]
    even = is_even()
    came = Received(even, ra, rb, None, None)
    lane = lane_iota()
    for p in range(planes):
        corner = jnp.where(lane < 2 * CORNER, came.x_high(p, 2), came.x_low(p, 2))
        for k in range(2):
            minus, plus = sources[p][2 + k], sources[p][4 + k]
            e_ref[p, k] = jnp.where(even, plus, minus)
            o_ref[p, k] = jnp.where(even, minus, plus)
        e_ref[p, 2] = corner
        o_ref[p, 2] = corner


TILE_CODES = tuple((t, t) for t in range(24)) + ((31, 24),)


def gather(table, index, codes):
    lane = index & (LANES - 1)
    code = index >> 7
    values = [jnp.zeros(index.shape, jnp.float32) for _ in range(DOF)]
    for c, t in codes:
        mask = code == c
        for d in range(DOF):
            row = jnp.broadcast_to(table[t, d : d + 1, :], index.shape)
            got = jnp.take_along_axis(row, lane, axis=1, mode="promise_in_bounds")
            values[d] = jnp.where(mask, got, values[d])
    return values


def relative(jac, values):
    out = []
    for k in range(ROWS):
        u = jac[k * DOF] * values[0]
        for d in range(1, DOF):
            u = u + jac[k * DOF + d] * values[d]
        out.append(u)
    return out


def middle_kernel(
    first, jac_a, jac_b, precond, bias, mu, stick, act, lam_in,
    id_a, id_b, hot_a, hot_b, own, halo, v_own, m_own, *refs,
):
    if first:
        ra, rb, qe, qo, lam_out, own_out, halo_out, xa, xb, v_halo, m_halo = refs[:11]
    else:
        v_halo, m_halo, ra, rb, qe, qo, lam_out, own_out, halo_out, xa, xb = refs[:11]
    table, force, left_a, left_b = refs[11:]
    even = is_even()
    came = Received(even, ra, rb, qe, qo)
    if first:
        for ref, p in ((v_halo, 2), (m_halo, 3)):
            for t, value in enumerate(came.plane(p)):
                ref[t] = value
    total = add_own(own, came.plane(1))
    total_halo = [a + b for a, b in zip([halo[t] for t in range(HALO_TILES)], came.plane(0))]
    for t in range(OWN_TILES):
        table[t] = v_own[t] + m_own[t] * total[t]
    for t in range(HALO_TILES):
        table[OWN_TILES + t] = v_halo[t] + m_halo[t] * total_halo[t]
    u_a = relative(jac_a, gather(table, id_a[...], TILE_CODES[:OWN_TILES]))
    u_b = relative(jac_b, gather(table, id_b[...], TILE_CODES))
    target = [u_a[k] + u_b[k] + bias[k] for k in range(ROWS)]
    active = act[...].astype(jnp.float32)
    if first:
        lam = [active * lam_in[k] for k in range(ROWS)]
    else:
        lam = [lam_in[k] for k in range(ROWS)]
    raw = []
    for k in range(ROWS):
        w = precond[k * ROWS] * target[0]
        for j in range(1, ROWS):
            w = w + precond[k * ROWS + j] * target[j]
        raw.append(lam[k] - w)
    normal = jnp.maximum(raw[0], 0.0)
    bound = mu[...] * (1.0 + 0.5 * stick[...].astype(jnp.float32)) * normal + 0.1
    square = raw[1] * raw[1] + raw[2] * raw[2]
    scale = bound / jnp.sqrt(jnp.maximum(square, bound * bound))
    lam = [active * normal, active * (raw[1] * scale), active * (raw[2] * scale)]
    for k in range(ROWS):
        lam_out[k] = lam[k]
    sums, sums_halo = scatter(lam, jac_a, jac_b, id_a, id_b, hot_a, hot_b, force, left_a, left_b)
    for t in range(OWN_TILES):
        own_out[t] = sums[t]
    for t in range(HALO_TILES):
        halo_out[t] = sums_halo[t]
    put_x(even, [sums, sums_halo], xa, xb)


def last_kernel(own, v_own, m_own, ra, rb, qe, qo, out):
    came = Received(is_even(), ra, rb, qe, qo)
    total = add_own(own, came.plane(1))
    from_tables([v_own[t] + m_own[t] * total[t] for t in range(OWN_TILES)], out)


def exchange_pairs(nx, ny):
    up = []
    for x in range(nx):
        for y in range(ny):
            to = x + 1 if y % 2 == 0 else x - 1
            goal = (to, y) if 0 <= to < nx else (x, y ^ 1)
            up.append((x * ny + y, goal[0] * ny + goal[1]))
    down = [(b, a) for a, b in up]
    near = [(y, y ^ 1) for y in range(ny)]
    far = [(y, (((y + 1) ^ 1) - 1) % ny) for y in range(ny)]
    return up, down, near, far


def on_device(
    velocity0, inv_mass, jac_a, jac_b, precond, bias, friction, impulse0, body_a, body_b, active, sticking
):
    nx, ny = lax.axis_size("gx"), lax.axis_size("gy")
    up, down, near, far = exchange_pairs(nx, ny)
    rows, lanes = body_a.shape[-2:]
    flat = lambda a: a.reshape(-1, rows, lanes)
    plain = lambda a: a.reshape(rows, lanes)
    jac_a, jac_b, precond, bias, impulse0 = map(flat, (jac_a, jac_b, precond, bias, impulse0))
    friction, body_a, body_b, active, sticking = map(plain, (friction, body_a, body_b, active, sticking))
    start, minv = (a.reshape(-1, lanes) for a in (velocity0, inv_mass))
    contacts = rows * lanes
    f32, i32, bf16 = jnp.float32, jnp.int32, jnp.bfloat16
    arr = jax.ShapeDtypeStruct
    vmem = pl.BlockSpec(memory_space=pltpu.VMEM)
    own_t, halo_t = arr((OWN_TILES, 8, lanes), f32), arr((HALO_TILES, 8, lanes), f32)
    lam_t = arr((ROWS, rows, lanes), f32)
    ids_t, hot_t = arr((rows, lanes), i32), arr((NBND, contacts), bf16)
    message = lambda p: arr((p, 3, 8, lanes), f32)
    work = [
        pltpu.VMEM((8 * rows, lanes), f32),
        pltpu.VMEM((16 * len(OWN_HEADS), contacts), bf16),
        pltpu.VMEM((16 * len(ALL_HEADS), contacts), bf16),
    ]
    table = [pltpu.VMEM((OWN_TILES + HALO_TILES, 8, lanes), f32)]

    def call(kernel, outs, scratch, name, *operands, space=pltpu.VMEM):
        return pl.pallas_call(
            kernel,
            out_shape=outs,
            in_specs=[pl.BlockSpec(memory_space=space)] * len(operands),
            out_specs=jax.tree.map(lambda _: vmem, outs),
            scratch_shapes=scratch,
            compiler_params=pltpu.CompilerParams(vmem_limit_bytes=32 * 1024 * 1024),
            name=name,
        )(*operands)

    def exchange(xa, xb, sources):
        planes = xa.shape[0]
        ra = lax.ppermute(xa, ("gx", "gy"), up)
        rb = lax.ppermute(xb, ("gx", "gy"), down)
        ye, yo = call(
            lambda *refs: turn_kernel(planes, *refs), (message(planes), message(planes)), [], "turn", ra, rb, *sources
        )
        return ra, rb, lax.ppermute(ye, "gy", near), lax.ppermute(yo, "gy", far)

    sources = (body_a, body_b, active, impulse0, jac_a, jac_b, start, minv, precond, bias, friction, sticking)
    like = lambda a: arr(a.shape, a.dtype)
    kept = (jac_a, jac_b, precond, bias, friction, sticking, active, impulse0)
    sources = [pltpu.with_memory_space_constraint(a, pltpu.HBM) for a in sources]
    made = call(
        first_kernel,
        (*map(like, kept), ids_t, ids_t, hot_t, hot_t, own_t, halo_t, own_t, own_t, message(4), message(4)),
        [pltpu.VMEM(a.shape, a.dtype) for a in (body_a, body_b, start, minv)]
        + work
        + [pltpu.SemaphoreType.DMA((len(sources),))],
        "first",
        *sources,
        space=pltpu.HBM,
    )
    fixed, lam = made[:7], made[7]
    id_a, id_b, hot_a, hot_b, own, halo, v_own, m_own, xa, xb = made[8:]
    for step in range(ITERS):
        first = step == 0
        sources = (own, halo, v_own, m_own) if first else (own, halo)
        received = exchange(xa, xb, sources)
        ins = (*fixed, lam, id_a, id_b, hot_a, hot_b, own, halo, v_own, m_own)
        outs = (lam_t, own_t, halo_t, message(2), message(2))
        kernel = lambda *refs, first=first: middle_kernel(first, *refs)
        if first:
            lam, own, halo, xa, xb, v_halo, m_halo = call(
                kernel, outs + (halo_t, halo_t), table + work, "middle0", *ins, *received
            )
        else:
            lam, own, halo, xa, xb = call(
                kernel, outs, table + work, "middle", *ins, v_halo, m_halo, *received
            )
    received = exchange(xa, xb, (own, halo))
    out = call(last_kernel, arr(start.shape, f32), [], "last", own, v_own, m_own, *received)
    return lam.reshape(ROWS, 1, 1, rows, lanes), out.reshape(velocity0.shape)


def solution(mesh):
    whole = ("groups", "gx")
    body = P(None, whole, "gy", None)
    many = P(None, whole, "gy", None, None)
    one = P(whole, "gy", None, None)
    return jax.shard_map(
        on_device,
        mesh=mesh,
        in_specs=(body, body, many, many, many, many, one, many, one, one, one, one),
        out_specs=(many, body),
        check_vma=False,
    )
```

```python
import jax
import jax.numpy as jnp
import numpy as np
from jax import lax
from jax.experimental import pallas as pl
from jax.experimental.pallas import tpu as pltpu
from jax.sharding import PartitionSpec as P

ROWS = 3
DOF = 6
ITERS = 3
LANES = 128
NB = 2048
NBND = 256
CORNER = NBND // 8
OWN_TILES = NB // LANES
EDGE_TILES = 2
HALO_TILES = 9
CORNER_TILE = OWN_TILES - 1
HALO_CORNER = HALO_TILES - 1
SET_START = (0, 32, 288, 320, 576, 832, 864, 1120)
TABLE_START = (1920, 0, 1952, 256, 512, 1984, 768, 2016)
INTERIOR_START = 1152
INTERIOR_TABLE = 1024
EDGE_SLOTS = (1, 3, 4, 6)
CORNER_SLOTS = (0, 2, 5, 7)


def table_index(body):
    steps = []
    for slot in range(8):
        steps.append((SET_START[slot], TABLE_START[slot] - SET_START[slot]))
    steps.append((INTERIOR_START, INTERIOR_TABLE - INTERIOR_START))
    for slot in range(8):
        steps.append((NB + slot * NBND, TABLE_START[slot] - slot * NBND))
    shift = jnp.full(body.shape, steps[0][1], jnp.int32)
    for start, delta in steps[1:]:
        shift = jnp.where(body >= start, delta, shift)
    return body + shift


def lane_iota():
    return lax.broadcasted_iota(jnp.int32, (8, LANES), 1)


def to_tables(ref):
    zero = jnp.zeros((2, LANES), jnp.float32)
    blocks = [
        jnp.concatenate([ref[pl.ds(k, DOF, stride=OWN_TILES), :], zero], axis=0)
        for k in range(OWN_TILES)
    ]
    lane = lane_iota()
    tiles = []
    for slot in EDGE_SLOTS:
        first, off = divmod(SET_START[slot], LANES)
        rolled = [pltpu.roll(blocks[first + j], LANES - off, 1) for j in range(3)]
        for j in range(2):
            tiles.append(jnp.where(lane < LANES - off, rolled[j], rolled[j + 1]))
    tiles += blocks[INTERIOR_START // LANES :]
    corner = jnp.zeros((8, LANES), jnp.float32)
    for place, slot in enumerate(CORNER_SLOTS):
        block = blocks[SET_START[slot] // LANES]
        corner = jnp.where(lane // CORNER == place, block, corner)
    tiles.append(corner)
    return tiles


def from_tables(tiles, out_ref):
    lane = lane_iota()
    blocks = [jnp.zeros((8, LANES), jnp.float32) for _ in range(INTERIOR_START // LANES)]
    for e, slot in enumerate(EDGE_SLOTS):
        first, off = divmod(SET_START[slot], LANES)
        rolled = [pltpu.roll(tiles[2 * e + j], off, 1) for j in range(2)]
        blocks[first] = jnp.where(lane >= off, rolled[0], blocks[first])
        blocks[first + 1] = jnp.where(lane >= off, rolled[1], rolled[0])
        blocks[first + 2] = jnp.where(lane < off, rolled[1], blocks[first + 2])
    for place, slot in enumerate(CORNER_SLOTS):
        k = SET_START[slot] // LANES
        blocks[k] = jnp.where(lane // CORNER == place, tiles[CORNER_TILE], blocks[k])
    blocks += tiles[8:CORNER_TILE]
    for k in range(OWN_TILES):
        out_ref[pl.ds(k, DOF, stride=OWN_TILES), :] = blocks[k][:DOF]


def row_of(ref, r):
    return ref[pl.ds(r, 1), :]


def build_onehot(index, onehot_ref):
    rows = index.shape[0]
    lane = (index & (NBND - 1)).astype(jnp.float32).T
    base = lax.broadcasted_iota(jnp.int32, (LANES, NBND), 1).astype(jnp.float32).astype(jnp.bfloat16)
    one, zero = jnp.ones((), jnp.bfloat16), jnp.zeros((), jnp.bfloat16)
    for r in range(rows):
        q = jnp.broadcast_to(lane[:, r : r + 1], (LANES, LANES)).astype(jnp.bfloat16)
        q = jnp.concatenate([q, q], axis=1)
        onehot_ref[r * LANES : (r + 1) * LANES, :] = jnp.where(base == q, one, zero)


def forces(lam, jac_ref, force_ref):
    rows = lam[0].shape[0]
    for d in range(DOF):
        f = jac_ref[d] * lam[0]
        f = f + jac_ref[DOF + d] * lam[1]
        f = f + jac_ref[2 * DOF + d] * lam[2]
        force_ref[d * rows : (d + 1) * rows, :] = f
    for d in range(DOF, 8):
        force_ref[d * rows : (d + 1) * rows, :] = jnp.zeros_like(f)


def spread(force_ref, index_ref, left_ref, heads):
    rows = index_ref.shape[0]
    for r in range(rows):
        f = force_ref[pl.ds(r, 8, stride=rows), :]
        hi = f.astype(jnp.bfloat16).astype(jnp.float32)
        lo = f - hi
        both = jnp.concatenate([hi, lo], axis=0)
        head = jnp.broadcast_to(row_of(index_ref, r) >> 8, (16, LANES))
        for k, h in enumerate(heads):
            left_ref[16 * k : 16 * (k + 1), r * LANES : (r + 1) * LANES] = jnp.where(
                head == h, both, 0.0
            ).astype(jnp.bfloat16)


OWN_HEADS = tuple(range(8))
ALL_HEADS = OWN_HEADS + (8, 9, 10, 11, 15)


def scatter(lam, jac_a, jac_b, id_a, id_b, hot_a, hot_b, force, left_a, left_b):
    contract = (((1,), (0,)), ((), ()))
    forces(lam, jac_a, force)
    spread(force, id_a, left_a, OWN_HEADS)
    sum_a = lax.dot_general(left_a[...], hot_a[...], contract, preferred_element_type=jnp.float32)
    forces(lam, jac_b, force)
    spread(force, id_b, left_b, ALL_HEADS)
    sum_b = lax.dot_general(left_b[...], hot_b[...], contract, preferred_element_type=jnp.float32)

    def tile(s, k, j):
        lanes = slice(j * LANES, (j + 1) * LANES)
        return s[16 * k : 16 * k + 8, lanes] + s[16 * k + 8 : 16 * k + 16, lanes]

    own = [tile(sum_a, t // 2, t % 2) + tile(sum_b, t // 2, t % 2) for t in range(OWN_TILES)]
    halo = [tile(sum_b, 8 + t // 2, t % 2) for t in range(8)] + [tile(sum_b, 12, 1)]
    return own, halo


def put_x(even, planes, a_ref, b_ref):
    high = lane_iota() >= 2 * CORNER
    for p, tiles in enumerate(planes):
        up = (tiles[6], tiles[7], jnp.where(high, tiles[-1], 0.0))
        down = (tiles[0], tiles[1], jnp.where(high, 0.0, tiles[-1]))
        for k in range(3):
            a_ref[p, k] = jnp.where(even, down[k], up[k])
            b_ref[p, k] = jnp.where(even, up[k], down[k])


def is_even():
    return lax.rem(lax.axis_index("gy"), 2) == 0


def corners_in(y_low, y_high, p):
    lane = lane_iota()
    odd = (lane & CORNER) != 0
    return jnp.where(odd, pltpu.roll(y_high(p, 2), 96, 1), pltpu.roll(y_low(p, 2), 32, 1))


class Received:
    def __init__(self, even, a_ref, b_ref, e_ref, o_ref):
        def pick(first, second):
            return lambda p, k: jnp.where(even, first[p, k], second[p, k])

        self.x_low, self.x_high = pick(b_ref, a_ref), pick(a_ref, b_ref)
        if e_ref is not None:
            self.y_high, self.y_low = pick(o_ref, e_ref), pick(e_ref, o_ref)

    def plane(self, p):
        tiles = []
        for side in (self.x_low, self.y_low, self.y_high, self.x_high):
            tiles += [side(p, 0), side(p, 1)]
        return tiles + [corners_in(self.y_low, self.y_high, p)]


def add_own(own, came):
    out = [own[t] + came[t] for t in range(8)]
    out += [own[t] for t in range(8, CORNER_TILE)]
    return out + [own[CORNER_TILE] + came[HALO_CORNER]]


def first_kernel(*refs):
    sources, kept, outs = refs[:12], refs[12:20], refs[20:30]
    body_a, body_b, start, minv, force, left_a, left_b, sems = refs[30:]
    id_a, id_b, hot_a, hot_b, own, halo, v_own, m_own, xa, xb = outs
    jac_a, jac_b, precond, bias, mu, stick, act, lam0 = kept
    goals = (body_a, body_b, act, lam0, jac_a, jac_b, start, minv, precond, bias, mu, stick)
    copies = [pltpu.make_async_copy(s, g, sems.at[k]) for k, (s, g) in enumerate(zip(sources, goals))]
    for copy in copies:
        copy.start()
    even = is_even()
    copies[0].wait()
    id_a[...] = table_index(body_a[...])
    build_onehot(id_a[...], hot_a)
    copies[1].wait()
    id_b[...] = table_index(body_b[...])
    build_onehot(id_b[...], hot_b)
    for copy in copies[2:6]:
        copy.wait()
    active = act[...].astype(jnp.float32)
    lam = [active * lam0[k] for k in range(ROWS)]
    sums, sums_halo = scatter(lam, jac_a, jac_b, id_a, id_b, hot_a, hot_b, force, left_a, left_b)
    for copy in copies[6:8]:
        copy.wait()
    v, m = to_tables(start), to_tables(minv)
    for t in range(OWN_TILES):
        own[t], v_own[t], m_own[t] = sums[t], v[t], m[t]
    for t in range(HALO_TILES):
        halo[t] = sums_halo[t]
    put_x(even, [sums, sums_halo, v, m], xa, xb)
    for copy in copies[8:]:
        copy.wait()


def turn_kernel(planes, ra, rb, *refs):
    sources, (e_ref, o_ref) = refs[:-2], refs[-2:]
    even = is_even()
    came = Received(even, ra, rb, None, None)
    lane = lane_iota()
    for p in range(planes):
        corner = jnp.where(lane < 2 * CORNER, came.x_high(p, 2), came.x_low(p, 2))
        for k in range(2):
            minus, plus = sources[p][2 + k], sources[p][4 + k]
            e_ref[p, k] = jnp.where(even, minus, plus)
            o_ref[p, k] = jnp.where(even, plus, minus)
        e_ref[p, 2] = corner
        o_ref[p, 2] = corner


TILE_CODES = tuple((t, t) for t in range(24)) + ((31, 24),)


def gather(table, index, codes):
    values = [[] for _ in range(DOF)]
    for g in range(0, index.shape[0], 8):
        lane = index[g : g + 8] & (LANES - 1)
        code = index[g : g + 8] >> 7
        part = [jnp.zeros(lane.shape, jnp.float32) for _ in range(DOF)]
        for c, t in codes:
            mask = code == c
            for d in range(DOF):
                row = jnp.broadcast_to(table[t, d : d + 1, :], lane.shape)
                got = jnp.take_along_axis(row, lane, axis=1, mode="promise_in_bounds")
                part[d] = jnp.where(mask, got, part[d])
        for d in range(DOF):
            values[d].append(part[d])
    return [jnp.concatenate(v, axis=0) for v in values]


def relative(jac, values):
    out = []
    for k in range(ROWS):
        u = jac[k * DOF] * values[0]
        for d in range(1, DOF):
            u = u + jac[k * DOF + d] * values[d]
        out.append(u)
    return out


def middle_kernel(
    first, jac_a, jac_b, precond, bias, mu, stick, act, lam_in,
    id_a, id_b, hot_a, hot_b, own, halo, v_own, m_own, *refs,
):
    if first:
        ra, rb, qe, qo, lam_out, own_out, halo_out, xa, xb, v_halo, m_halo = refs[:11]
    else:
        v_halo, m_halo, ra, rb, qe, qo, lam_out, own_out, halo_out, xa, xb = refs[:11]
    table, force, left_a, left_b = refs[11:]
    even = is_even()
    came = Received(even, ra, rb, qe, qo)
    if first:
        for ref, p in ((v_halo, 2), (m_halo, 3)):
            for t, value in enumerate(came.plane(p)):
                ref[t] = value
    total = add_own(own, came.plane(1))
    total_halo = [a + b for a, b in zip([halo[t] for t in range(HALO_TILES)], came.plane(0))]
    for t in range(OWN_TILES):
        table[t] = v_own[t] + m_own[t] * total[t]
    for t in range(HALO_TILES):
        table[OWN_TILES + t] = v_halo[t] + m_halo[t] * total_halo[t]
    u_a = relative(jac_a, gather(table, id_a[...], TILE_CODES[:OWN_TILES]))
    u_b = relative(jac_b, gather(table, id_b[...], TILE_CODES))
    target = [u_a[k] + u_b[k] + bias[k] for k in range(ROWS)]
    active = act[...].astype(jnp.float32)
    if first:
        lam = [active * lam_in[k] for k in range(ROWS)]
    else:
        lam = [lam_in[k] for k in range(ROWS)]
    raw = []
    for k in range(ROWS):
        w = precond[k * ROWS] * target[0]
        for j in range(1, ROWS):
            w = w + precond[k * ROWS + j] * target[j]
        raw.append(lam[k] - w)
    normal = jnp.maximum(raw[0], 0.0)
    bound = mu[...] * (1.0 + 0.5 * stick[...].astype(jnp.float32)) * normal + 0.1
    square = raw[1] * raw[1] + raw[2] * raw[2]
    scale = bound / jnp.sqrt(jnp.maximum(square, bound * bound))
    lam = [active * normal, active * (raw[1] * scale), active * (raw[2] * scale)]
    for k in range(ROWS):
        lam_out[k] = lam[k]
    sums, sums_halo = scatter(lam, jac_a, jac_b, id_a, id_b, hot_a, hot_b, force, left_a, left_b)
    for t in range(OWN_TILES):
        own_out[t] = sums[t]
    for t in range(HALO_TILES):
        halo_out[t] = sums_halo[t]
    put_x(even, [sums, sums_halo], xa, xb)


def last_kernel(own, v_own, m_own, ra, rb, qe, qo, out):
    came = Received(is_even(), ra, rb, qe, qo)
    total = add_own(own, came.plane(1))
    from_tables([v_own[t] + m_own[t] * total[t] for t in range(OWN_TILES)], out)


def exchange_pairs(nx, ny):
    up = []
    for x in range(nx):
        for y in range(ny):
            to = x + 1 if y % 2 == 1 else x - 1
            goal = (to, y) if 0 <= to < nx else (x, y ^ 1)
            up.append((x * ny + y, goal[0] * ny + goal[1]))
    down = [(b, a) for a, b in up]
    near = [(y, y ^ 1) for y in range(ny)]
    far = [(y, (((y + 1) ^ 1) - 1) % ny) for y in range(ny)]
    return up, down, near, far


def on_device(
    velocity0, inv_mass, jac_a, jac_b, precond, bias, friction, impulse0, body_a, body_b, active, sticking
):
    nx, ny = lax.axis_size("gx"), lax.axis_size("gy")
    up, down, near, far = exchange_pairs(nx, ny)
    rows, lanes = body_a.shape[-2:]
    flat = lambda a: a.reshape(-1, rows, lanes)
    plain = lambda a: a.reshape(rows, lanes)
    jac_a, jac_b, precond, bias, impulse0 = map(flat, (jac_a, jac_b, precond, bias, impulse0))
    friction, body_a, body_b, active, sticking = map(plain, (friction, body_a, body_b, active, sticking))
    start, minv = (a.reshape(-1, lanes) for a in (velocity0, inv_mass))
    contacts = rows * lanes
    f32, i32, bf16 = jnp.float32, jnp.int32, jnp.bfloat16
    arr = jax.ShapeDtypeStruct
    vmem = pl.BlockSpec(memory_space=pltpu.VMEM)
    own_t, halo_t = arr((OWN_TILES, 8, lanes), f32), arr((HALO_TILES, 8, lanes), f32)
    lam_t = arr((ROWS, rows, lanes), f32)
    ids_t, hot_t = arr((rows, lanes), i32), arr((contacts, NBND), bf16)
    message = lambda p: arr((p, 3, 8, lanes), f32)
    work = [
        pltpu.VMEM((8 * rows, lanes), f32),
        pltpu.VMEM((16 * len(OWN_HEADS), contacts), bf16),
        pltpu.VMEM((16 * len(ALL_HEADS), contacts), bf16),
    ]
    table = [pltpu.VMEM((OWN_TILES + HALO_TILES, 8, lanes), f32)]

    def call(kernel, outs, scratch, name, *operands, space=pltpu.VMEM):
        return pl.pallas_call(
            kernel,
            out_shape=outs,
            in_specs=[pl.BlockSpec(memory_space=space)] * len(operands),
            out_specs=jax.tree.map(lambda _: vmem, outs),
            scratch_shapes=scratch,
            compiler_params=pltpu.CompilerParams(vmem_limit_bytes=32 * 1024 * 1024),
            name=name,
        )(*operands)

    def exchange(xa, xb, sources):
        planes = xa.shape[0]
        ra = lax.ppermute(xa, ("gx", "gy"), up)
        rb = lax.ppermute(xb, ("gx", "gy"), down)
        ye, yo = call(
            lambda *refs: turn_kernel(planes, *refs), (message(planes), message(planes)), [], "turn", ra, rb, *sources
        )
        return ra, rb, lax.ppermute(ye, "gy", far), lax.ppermute(yo, "gy", near)

    sources = (body_a, body_b, active, impulse0, jac_a, jac_b, start, minv, precond, bias, friction, sticking)
    like = lambda a: arr(a.shape, a.dtype)
    kept = (jac_a, jac_b, precond, bias, friction, sticking, active, impulse0)
    sources = [pltpu.with_memory_space_constraint(a, pltpu.HBM) for a in sources]
    made = call(
        first_kernel,
        (*map(like, kept), ids_t, ids_t, hot_t, hot_t, own_t, halo_t, own_t, own_t, message(4), message(4)),
        [pltpu.VMEM(a.shape, a.dtype) for a in (body_a, body_b, start, minv)]
        + work
        + [pltpu.SemaphoreType.DMA((len(sources),))],
        "first",
        *sources,
        space=pltpu.HBM,
    )
    fixed, lam = made[:7], made[7]
    id_a, id_b, hot_a, hot_b, own, halo, v_own, m_own, xa, xb = made[8:]
    for step in range(ITERS):
        first = step == 0
        sources = (own, halo, v_own, m_own) if first else (own, halo)
        received = exchange(xa, xb, sources)
        ins = (*fixed, lam, id_a, id_b, hot_a, hot_b, own, halo, v_own, m_own)
        outs = (lam_t, own_t, halo_t, message(2), message(2))
        kernel = lambda *refs, first=first: middle_kernel(first, *refs)
        if first:
            lam, own, halo, xa, xb, v_halo, m_halo = call(
                kernel, outs + (halo_t, halo_t), table + work, "middle0", *ins, *received
            )
        else:
            lam, own, halo, xa, xb = call(
                kernel, outs, table + work, "middle", *ins, v_halo, m_halo, *received
            )
    received = exchange(xa, xb, (own, halo))
    out = call(last_kernel, arr(start.shape, f32), [], "last", own, v_own, m_own, *received)
    return lam.reshape(ROWS, 1, 1, rows, lanes), out.reshape(velocity0.shape)


def solution(mesh):
    whole = ("groups", "gx")
    body = P(None, whole, "gy", None)
    many = P(None, whole, "gy", None, None)
    one = P(whole, "gy", None, None)
    return jax.shard_map(
        on_device,
        mesh=mesh,
        in_specs=(body, body, many, many, many, many, one, many, one, one, one, one),
        out_specs=(many, body),
        check_vma=False,
    )
```

```python
import jax
import jax.numpy as jnp
import numpy as np
from jax import lax
from jax.experimental import pallas as pl
from jax.experimental.pallas import tpu as pltpu
from jax.sharding import PartitionSpec as P

ROWS = 3
DOF = 6
ITERS = 3
LANES = 128
NB = 2048
NBND = 256
CORNER = NBND // 8
OWN_TILES = NB // LANES
EDGE_TILES = 2
HALO_TILES = 9
CORNER_TILE = OWN_TILES - 1
HALO_CORNER = HALO_TILES - 1
SET_START = (0, 32, 288, 320, 576, 832, 864, 1120)
TABLE_START = (1920, 0, 1952, 256, 512, 1984, 768, 2016)
INTERIOR_START = 1152
INTERIOR_TABLE = 1024
EDGE_SLOTS = (1, 3, 4, 6)
CORNER_SLOTS = (0, 2, 5, 7)


def table_index(body):
    steps = []
    for slot in range(8):
        steps.append((SET_START[slot], TABLE_START[slot] - SET_START[slot]))
    steps.append((INTERIOR_START, INTERIOR_TABLE - INTERIOR_START))
    for slot in range(8):
        steps.append((NB + slot * NBND, TABLE_START[slot] - slot * NBND))
    shift = jnp.full(body.shape, steps[0][1], jnp.int32)
    for start, delta in steps[1:]:
        shift = jnp.where(body >= start, delta, shift)
    return body + shift


def lane_iota():
    return lax.broadcasted_iota(jnp.int32, (8, LANES), 1)


def to_tables(ref):
    zero = jnp.zeros((2, LANES), jnp.float32)
    blocks = [
        jnp.concatenate([ref[pl.ds(k, DOF, stride=OWN_TILES), :], zero], axis=0)
        for k in range(OWN_TILES)
    ]
    lane = lane_iota()
    tiles = []
    for slot in EDGE_SLOTS:
        first, off = divmod(SET_START[slot], LANES)
        rolled = [pltpu.roll(blocks[first + j], LANES - off, 1) for j in range(3)]
        for j in range(2):
            tiles.append(jnp.where(lane < LANES - off, rolled[j], rolled[j + 1]))
    tiles += blocks[INTERIOR_START // LANES :]
    corner = jnp.zeros((8, LANES), jnp.float32)
    for place, slot in enumerate(CORNER_SLOTS):
        block = blocks[SET_START[slot] // LANES]
        corner = jnp.where(lane // CORNER == place, block, corner)
    tiles.append(corner)
    return tiles


def from_tables(tiles, out_ref):
    lane = lane_iota()
    blocks = [jnp.zeros((8, LANES), jnp.float32) for _ in range(INTERIOR_START // LANES)]
    for e, slot in enumerate(EDGE_SLOTS):
        first, off = divmod(SET_START[slot], LANES)
        rolled = [pltpu.roll(tiles[2 * e + j], off, 1) for j in range(2)]
        blocks[first] = jnp.where(lane >= off, rolled[0], blocks[first])
        blocks[first + 1] = jnp.where(lane >= off, rolled[1], rolled[0])
        blocks[first + 2] = jnp.where(lane < off, rolled[1], blocks[first + 2])
    for place, slot in enumerate(CORNER_SLOTS):
        k = SET_START[slot] // LANES
        blocks[k] = jnp.where(lane // CORNER == place, tiles[CORNER_TILE], blocks[k])
    blocks += tiles[8:CORNER_TILE]
    for k in range(OWN_TILES):
        out_ref[pl.ds(k, DOF, stride=OWN_TILES), :] = blocks[k][:DOF]


def row_of(ref, r):
    return ref[pl.ds(r, 1), :]


def build_onehot(index, onehot_ref):
    rows = index.shape[0]
    lane = (index & (NBND - 1)).astype(jnp.float32).T
    base = lax.broadcasted_iota(jnp.int32, (LANES, NBND), 1).astype(jnp.float32).astype(jnp.bfloat16)
    one, zero = jnp.ones((), jnp.bfloat16), jnp.zeros((), jnp.bfloat16)
    for r in range(rows):
        q = jnp.broadcast_to(lane[:, r : r + 1], (LANES, LANES)).astype(jnp.bfloat16)
        q = jnp.concatenate([q, q], axis=1)
        onehot_ref[r * LANES : (r + 1) * LANES, :] = jnp.where(base == q, one, zero)


def forces(lam, jac_ref, force_ref):
    rows = lam[0].shape[0]
    for d in range(DOF):
        f = jac_ref[d] * lam[0]
        f = f + jac_ref[DOF + d] * lam[1]
        f = f + jac_ref[2 * DOF + d] * lam[2]
        force_ref[d * rows : (d + 1) * rows, :] = f
    for d in range(DOF, 8):
        force_ref[d * rows : (d + 1) * rows, :] = jnp.zeros_like(f)


def spread(force_ref, index_ref, left_ref, heads):
    rows = index_ref.shape[0]
    for r in range(rows):
        f = force_ref[pl.ds(r, 8, stride=rows), :]
        hi = f.astype(jnp.bfloat16).astype(jnp.float32)
        lo = f - hi
        both = jnp.concatenate([hi, lo], axis=0)
        head = jnp.broadcast_to(row_of(index_ref, r) >> 8, (16, LANES))
        for k, h in enumerate(heads):
            left_ref[16 * k : 16 * (k + 1), r * LANES : (r + 1) * LANES] = jnp.where(
                head == h, both, 0.0
            ).astype(jnp.bfloat16)


OWN_HEADS = tuple(range(8))
ALL_HEADS = OWN_HEADS + (8, 9, 10, 11, 15)


def scatter(lam, jac_a, jac_b, id_a, id_b, hot_a, hot_b, force, left_a, left_b):
    contract = (((1,), (0,)), ((), ()))
    forces(lam, jac_a, force)
    spread(force, id_a, left_a, OWN_HEADS)
    sum_a = lax.dot_general(left_a[...], hot_a[...], contract, preferred_element_type=jnp.float32)
    forces(lam, jac_b, force)
    spread(force, id_b, left_b, ALL_HEADS)
    sum_b = lax.dot_general(left_b[...], hot_b[...], contract, preferred_element_type=jnp.float32)

    def tile(s, k, j):
        lanes = slice(j * LANES, (j + 1) * LANES)
        return s[16 * k : 16 * k + 8, lanes] + s[16 * k + 8 : 16 * k + 16, lanes]

    own = [tile(sum_a, t // 2, t % 2) + tile(sum_b, t // 2, t % 2) for t in range(OWN_TILES)]
    halo = [tile(sum_b, 8 + t // 2, t % 2) for t in range(8)] + [tile(sum_b, 12, 1)]
    return own, halo


def is_even():
    return lax.rem(lax.axis_index("gy"), 2) == 0


GROUP = 32
LAST_GROUP = 24


def put_tiles(ref, base, tiles, end):
    for k, tile in enumerate(tiles):
        ref[base + DOF * k : base + DOF * (k + 1), :] = tile[:DOF]
    rest = DOF * len(tiles)
    ref[base + rest : base + end, :] = jnp.zeros((end - rest, LANES), jnp.float32)


def put_x(even, groups, a_ref, b_ref):
    high = lane_iota() >= 2 * CORNER
    for g, (first, second) in enumerate(groups):
        half = jnp.zeros_like(second[-1]) if first is None else first[-1]
        up = [second[6], second[7], jnp.where(high, second[-1], pltpu.roll(half, 2 * CORNER, 1))]
        down = [second[0], second[1], jnp.where(high, pltpu.roll(second[-1], 2 * CORNER, 1), half)]
        if first is not None:
            up, down = [first[6], first[7]] + up, [first[0], first[1]] + down
        rows = a_ref.shape[0] // len(groups)
        put_tiles(a_ref, g * rows, [jnp.where(even, d, u) for u, d in zip(up, down)], rows)
        put_tiles(b_ref, g * rows, [jnp.where(even, u, d) for u, d in zip(up, down)], rows)


class Received:
    def __init__(self, even, a_ref, b_ref, e_ref=None, o_ref=None):
        def pick(when, other):
            def tile(row):
                return jnp.where(even, when[pl.ds(row, 8), :], other[pl.ds(row, 8), :])

            return tile

        self.rows = GROUP if a_ref.shape[0] % GROUP == 0 else LAST_GROUP
        self.tiles = 5 if self.rows == GROUP else 3
        self.x_low, self.x_high = pick(b_ref, a_ref), pick(a_ref, b_ref)
        if e_ref is not None:
            self.y_low, self.y_high = pick(e_ref, o_ref), pick(o_ref, e_ref)

    def edge(self, side, plane):
        place = 2 * (plane % 2) if self.tiles == 5 else 0
        base = self.rows * (plane // 2) + DOF * place
        return [side(base), side(base + DOF)]

    def corner_row(self, plane):
        return self.rows * (plane // 2) + DOF * (self.tiles - 1)

    def x_corner(self, plane):
        lane = lane_iota()
        low, high = self.x_low(self.corner_row(plane)), self.x_high(self.corner_row(plane))
        left = lane < 2 * CORNER
        first = jnp.where(left, high, pltpu.roll(low, 2 * CORNER, 1))
        second = jnp.where(left, pltpu.roll(high, 2 * CORNER, 1), low)
        odd = (lane & CORNER) != 0
        minus = jnp.where(odd, pltpu.roll(second, CORNER, 1), first)
        plus = jnp.where(odd, first, pltpu.roll(second, 3 * CORNER, 1))
        return minus, plus

    def corner(self, plane):
        odd = (lane_iota() & CORNER) != 0
        low, high = self.y_low(self.corner_row(plane)), self.y_high(self.corner_row(plane))
        if plane % 2:
            return pltpu.roll(jnp.where(odd, high, low), 2 * CORNER, 1)
        return jnp.where(odd, pltpu.roll(high, 3 * CORNER, 1), pltpu.roll(low, CORNER, 1))


X_EDGES = (0, 1, 6, 7)
Y_EDGES = (2, 3, 4, 5)
INTERIOR = tuple(range(8, CORNER_TILE))


def x_plane(came, plane):
    low, high = came.edge(came.x_low, plane), came.edge(came.x_high, plane)
    return dict(zip(X_EDGES, low + high))


def y_plane(came, plane):
    low, high = came.edge(came.y_low, plane), came.edge(came.y_high, plane)
    return dict(zip(Y_EDGES, low + high))


def first_kernel(*refs):
    sources, kept, outs = refs[:12], refs[12:20], refs[20:30]
    body_a, body_b, start, minv, force, left_a, left_b, sems = refs[30:]
    id_a, id_b, hot_a, hot_b, own, halo, v_own, m_own, xa, xb = outs
    jac_a, jac_b, precond, bias, mu, stick, act, lam0 = kept
    goals = (body_a, body_b, act, lam0, jac_a, jac_b, start, minv, precond, bias, mu, stick)
    copies = [pltpu.make_async_copy(s, g, sems.at[k]) for k, (s, g) in enumerate(zip(sources, goals))]
    for copy in copies:
        copy.start()
    even = is_even()
    copies[0].wait()
    id_a[...] = table_index(body_a[...])
    build_onehot(id_a[...], hot_a)
    copies[1].wait()
    id_b[...] = table_index(body_b[...])
    build_onehot(id_b[...], hot_b)
    for copy in copies[2:6]:
        copy.wait()
    active = act[...].astype(jnp.float32)
    lam = [active * lam0[k] for k in range(ROWS)]
    sums, sums_halo = scatter(lam, jac_a, jac_b, id_a, id_b, hot_a, hot_b, force, left_a, left_b)
    for copy in copies[6:8]:
        copy.wait()
    v, m = to_tables(start), to_tables(minv)
    for t in range(OWN_TILES):
        own[t], v_own[t], m_own[t] = sums[t], v[t], m[t]
    for t in range(HALO_TILES):
        halo[t] = sums_halo[t]
    put_x(even, [(sums, sums_halo), (v, m)], xa, xb)
    for copy in copies[8:]:
        copy.wait()


def turn_kernel(ra, rb, *refs):
    sources, (e_ref, o_ref) = refs[:-2], refs[-2:]
    even = is_even()
    came = Received(even, ra, rb)
    groups = ra.shape[0] // came.rows
    for g in range(groups):
        planes = sources[2 * g : 2 * g + 2] if len(sources) > 1 else sources
        minus = [p[t] for p in planes for t in (2, 3)]
        plus = [p[t] for p in planes for t in (4, 5)]
        corner = came.x_corner(2 * g)
        minus, plus = minus + [corner[0]], plus + [corner[1]]
        put_tiles(e_ref, g * came.rows, [jnp.where(even, m, p) for m, p in zip(minus, plus)], came.rows)
        put_tiles(o_ref, g * came.rows, [jnp.where(even, p, m) for m, p in zip(minus, plus)], came.rows)


def gather(table, index, codes, start=None):
    values = [[] for _ in range(DOF)]
    for g in range(0, index.shape[0], 8):
        lane = index[g : g + 8] & (LANES - 1)
        code = index[g : g + 8] >> 7
        if start is None:
            part = [jnp.zeros(lane.shape, jnp.float32) for _ in range(DOF)]
        else:
            part = [start[d, g : g + 8, :] for d in range(DOF)]
        for c, t in codes:
            mask = code == c
            for d in range(DOF):
                row = jnp.broadcast_to(table[t, d : d + 1, :], lane.shape)
                got = jnp.take_along_axis(row, lane, axis=1, mode="promise_in_bounds")
                part[d] = jnp.where(mask, got, part[d])
        for d in range(DOF):
            values[d].append(part[d])
    return [jnp.concatenate(v, axis=0) for v in values]


def own_codes(tiles):
    return tuple((t, t) for t in tiles)


def halo_codes(tiles):
    return tuple((OWN_TILES + (15 if t == HALO_CORNER else t), OWN_TILES + t) for t in tiles)


def gather_both(table, id_a, id_b, own_tiles, halo_tiles, out, start):
    part = (None, None) if start is None else (start.at[:DOF], start.at[DOF:])
    for ref, ids, codes, first, base in (
        (out, id_a, own_codes(own_tiles), part[0], 0),
        (out, id_b, own_codes(own_tiles) + halo_codes(halo_tiles), part[1], DOF),
    ):
        for d, value in enumerate(gather(table, ids[...], codes, first)):
            ref[base + d] = value


def inner_kernel(own, v_own, m_own, id_a, id_b, out, table):
    for t in INTERIOR:
        table[t] = v_own[t] + m_own[t] * own[t]
    gather_both(table, id_a, id_b, INTERIOR, (), out, None)


def side_kernel(first, own, halo, v_own, m_own, id_a, id_b, part, ra, rb, *refs):
    v_halo, m_halo, (out, table) = (None, None, refs) if first else (refs[0], refs[1], refs[2:])
    came = Received(is_even(), ra, rb)
    theirs, ours = x_plane(came, 0), x_plane(came, 1)
    if first:
        v_halo, m_halo = x_plane(came, 2), x_plane(came, 3)
    for t in X_EDGES:
        table[t] = v_own[t] + m_own[t] * (own[t] + ours[t])
        table[OWN_TILES + t] = v_halo[t] + m_halo[t] * (halo[t] + theirs[t])
    gather_both(table, id_a, id_b, X_EDGES, X_EDGES, out, part)


def relative(jac, values):
    out = []
    for k in range(ROWS):
        u = jac[k * DOF] * values[0]
        for d in range(1, DOF):
            u = u + jac[k * DOF + d] * values[d]
        out.append(u)
    return out


def middle_kernel(
    first, last, jac_a, jac_b, precond, bias, mu, stick, act, lam_in,
    id_a, id_b, hot_a, hot_b, own, halo, v_own, m_own, part, ra, rb, qe, qo, *refs,
):
    if first:
        lam_out, own_out, halo_out, xa, xb, v_halo, m_halo = refs[:7]
    else:
        v_halo, m_halo, lam_out, own_out, halo_out, xa, xb = refs[:7]
    table, force, left_a, left_b = refs[7:]
    even = is_even()
    came = Received(even, ra, rb, qe, qo)
    if first:
        for ref, p in ((v_halo, 2), (m_halo, 3)):
            for t, value in (x_plane(came, p) | y_plane(came, p)).items():
                ref[t] = value
            ref[HALO_CORNER] = came.corner(p)
    theirs, ours = y_plane(came, 0), y_plane(came, 1)
    theirs[HALO_CORNER], ours[CORNER_TILE] = came.corner(0), came.corner(1)
    for t, value in ours.items():
        table[t] = v_own[t] + m_own[t] * (own[t] + value)
    for t, value in theirs.items():
        table[OWN_TILES + t] = v_halo[t] + m_halo[t] * (halo[t] + value)
    late, late_halo = own_codes(ours), halo_codes(theirs)
    v_a = gather(table, id_a[...], late, part.at[:DOF])
    v_b = gather(table, id_b[...], late + late_halo, part.at[DOF:])
    u_a = relative(jac_a, v_a)
    u_b = relative(jac_b, v_b)
    target = [u_a[k] + u_b[k] + bias[k] for k in range(ROWS)]
    active = act[...].astype(jnp.float32)
    if first:
        lam = [active * lam_in[k] for k in range(ROWS)]
    else:
        lam = [lam_in[k] for k in range(ROWS)]
    raw = []
    for k in range(ROWS):
        w = precond[k * ROWS] * target[0]
        for j in range(1, ROWS):
            w = w + precond[k * ROWS + j] * target[j]
        raw.append(lam[k] - w)
    normal = jnp.maximum(raw[0], 0.0)
    bound = mu[...] * (1.0 + 0.5 * stick[...].astype(jnp.float32)) * normal + 0.1
    square = raw[1] * raw[1] + raw[2] * raw[2]
    scale = bound / jnp.sqrt(jnp.maximum(square, bound * bound))
    lam = [active * normal, active * (raw[1] * scale), active * (raw[2] * scale)]
    for k in range(ROWS):
        lam_out[k] = lam[k]
    sums, sums_halo = scatter(lam, jac_a, jac_b, id_a, id_b, hot_a, hot_b, force, left_a, left_b)
    for t in range(OWN_TILES):
        own_out[t] = sums[t]
    for t in range(HALO_TILES):
        halo_out[t] = sums_halo[t]
    put_x(even, [(None if last else sums, sums_halo)], xa, xb)


def keep_kernel(lam, out, sem):
    copy = pltpu.make_async_copy(lam, out, sem)
    copy.start()
    copy.wait()


def last_kernel(own, v_own, m_own, ra, rb, qe, qo, out):
    came = Received(is_even(), ra, rb, qe, qo)
    ours = x_plane(came, 1) | y_plane(came, 1)
    ours[CORNER_TILE] = came.corner(1)
    total = [own[t] + ours[t] if t in ours else own[t] for t in range(OWN_TILES)]
    from_tables([v_own[t] + m_own[t] * total[t] for t in range(OWN_TILES)], out)


def exchange_pairs(nx, ny):
    up = []
    for x in range(nx):
        for y in range(ny):
            to = x + 1 if y % 2 == 1 else x - 1
            goal = (to, y) if 0 <= to < nx else (x, y ^ 1)
            up.append((x * ny + y, goal[0] * ny + goal[1]))
    down = [(b, a) for a, b in up]
    near = [(y, y ^ 1) for y in range(ny)]
    far = [(y, (((y + 1) ^ 1) - 1) % ny) for y in range(ny)]
    return up, down, near, far


def on_device(
    velocity0, inv_mass, jac_a, jac_b, precond, bias, friction, impulse0, body_a, body_b, active, sticking
):
    nx, ny = lax.axis_size("gx"), lax.axis_size("gy")
    up, down, near, far = exchange_pairs(nx, ny)
    rows, lanes = body_a.shape[-2:]
    flat = lambda a: a.reshape(-1, rows, lanes)
    plain = lambda a: a.reshape(rows, lanes)
    jac_a, jac_b, precond, bias, impulse0 = map(flat, (jac_a, jac_b, precond, bias, impulse0))
    friction, body_a, body_b, active, sticking = map(plain, (friction, body_a, body_b, active, sticking))
    start, minv = (a.reshape(-1, lanes) for a in (velocity0, inv_mass))
    contacts = rows * lanes
    f32, i32, bf16 = jnp.float32, jnp.int32, jnp.bfloat16
    arr = jax.ShapeDtypeStruct
    vmem = pl.BlockSpec(memory_space=pltpu.VMEM)
    own_t, halo_t = arr((OWN_TILES, 8, lanes), f32), arr((HALO_TILES, 8, lanes), f32)
    lam_t = arr((ROWS, rows, lanes), f32)
    ids_t, hot_t = arr((rows, lanes), i32), arr((contacts, NBND), bf16)
    message = lambda r: arr((r, lanes), f32)
    work = [
        pltpu.VMEM((8 * rows, lanes), f32),
        pltpu.VMEM((16 * len(OWN_HEADS), contacts), bf16),
        pltpu.VMEM((16 * len(ALL_HEADS), contacts), bf16),
    ]
    table = [pltpu.VMEM((OWN_TILES + HALO_TILES, 8, lanes), f32)]

    def call(kernel, outs, scratch, name, *operands, space=pltpu.VMEM, out_space=pltpu.VMEM):
        return pl.pallas_call(
            kernel,
            out_shape=outs,
            in_specs=[pl.BlockSpec(memory_space=space)] * len(operands),
            out_specs=jax.tree.map(lambda _: pl.BlockSpec(memory_space=out_space), outs),
            scratch_shapes=scratch,
            compiler_params=pltpu.CompilerParams(vmem_limit_bytes=32 * 1024 * 1024),
            name=name,
        )(*operands)

    def along_x(xa, xb):
        return lax.ppermute(xa, ("gx", "gy"), up), lax.ppermute(xb, ("gx", "gy"), down)

    def along_y(ra, rb, sources):
        like = arr(ra.shape, f32)
        ye, yo = call(turn_kernel, (like, like), [], "turn", ra, rb, *sources)
        return lax.ppermute(ye, "gy", far), lax.ppermute(yo, "gy", near)

    sources = (body_a, body_b, active, impulse0, jac_a, jac_b, start, minv, precond, bias, friction, sticking)
    like = lambda a: arr(a.shape, a.dtype)
    kept = (jac_a, jac_b, precond, bias, friction, sticking, active, impulse0)
    sources = [pltpu.with_memory_space_constraint(a, pltpu.HBM) for a in sources]
    made = call(
        first_kernel,
        (*map(like, kept), ids_t, ids_t, hot_t, hot_t, own_t, halo_t, own_t, own_t, message(2 * GROUP), message(2 * GROUP)),
        [pltpu.VMEM(a.shape, a.dtype) for a in (body_a, body_b, start, minv)]
        + work
        + [pltpu.SemaphoreType.DMA((len(sources),))],
        "first",
        *sources,
        space=pltpu.HBM,
    )
    fixed, lam = made[:7], made[7]
    id_a, id_b, hot_a, hot_b, own, halo, v_own, m_own, xa, xb = made[8:]
    part_t = arr((2 * DOF, rows, lanes), f32)
    halo_tables = ()
    for step in range(ITERS):
        first, last = step == 0, step == ITERS - 1
        came_x = along_x(xa, xb)
        part = call(inner_kernel, part_t, table, "inner", own, v_own, m_own, id_a, id_b)
        came_y = along_y(*came_x, (own, halo, v_own, m_own) if first else (own, halo))
        part = call(
            lambda *refs, first=first: side_kernel(first, *refs), part_t, table, "side",
            own, halo, v_own, m_own, id_a, id_b, part, *came_x, *halo_tables,
        )
        sent = message(LAST_GROUP if last else GROUP)
        outs = (lam_t, own_t, halo_t, sent, sent) + ((halo_t, halo_t) if first else ())
        lam, own, halo, xa, xb, *made = call(
            lambda *refs, first=first, last=last: middle_kernel(first, last, *refs), outs, table + work, "middle",
            *fixed, lam, id_a, id_b, hot_a, hot_b, own, halo, v_own, m_own, part, *came_x, *came_y, *halo_tables,
        )
        halo_tables = tuple(made) or halo_tables
    came_x = along_x(xa, xb)
    lam = call(keep_kernel, lam_t, [pltpu.SemaphoreType.DMA], "keep", lam, out_space=pltpu.HBM)
    came_y = along_y(*came_x, (halo,))
    out = call(last_kernel, arr(start.shape, f32), [], "last", own, v_own, m_own, *came_x, *came_y)
    return lam.reshape(ROWS, 1, 1, rows, lanes), out.reshape(velocity0.shape)


def solution(mesh):
    whole = ("groups", "gx")
    body = P(None, whole, "gy", None)
    many = P(None, whole, "gy", None, None)
    one = P(whole, "gy", None, None)
    return jax.shard_map(
        on_device,
        mesh=mesh,
        in_specs=(body, body, many, many, many, many, one, many, one, one, one, one),
        out_specs=(many, body),
        check_vma=False,
    )
```

```python
import jax
import jax.numpy as jnp
import numpy as np
from jax import lax
from jax.experimental import pallas as pl
from jax.experimental.pallas import tpu as pltpu
from jax.sharding import PartitionSpec as P

ROWS = 3
DOF = 6
ITERS = 3
LANES = 128
NB = 2048
NBND = 256
CORNER = NBND // 8
OWN_TILES = NB // LANES
EDGE_TILES = 2
HALO_TILES = 9
CORNER_TILE = OWN_TILES - 1
HALO_CORNER = HALO_TILES - 1
SET_START = (0, 32, 288, 320, 576, 832, 864, 1120)
TABLE_START = (1920, 0, 1952, 256, 512, 1984, 768, 2016)
INTERIOR_START = 1152
INTERIOR_TABLE = 1024
EDGE_SLOTS = (1, 3, 4, 6)
CORNER_SLOTS = (0, 2, 5, 7)


def table_index(body):
    steps = []
    for slot in range(8):
        steps.append((SET_START[slot], TABLE_START[slot] - SET_START[slot]))
    steps.append((INTERIOR_START, INTERIOR_TABLE - INTERIOR_START))
    for slot in range(8):
        steps.append((NB + slot * NBND, TABLE_START[slot] - slot * NBND))
    shift = jnp.full(body.shape, steps[0][1], jnp.int32)
    for start, delta in steps[1:]:
        shift = jnp.where(body >= start, delta, shift)
    return body + shift


def lane_iota():
    return lax.broadcasted_iota(jnp.int32, (8, LANES), 1)


def to_tables(ref):
    zero = jnp.zeros((2, LANES), jnp.float32)
    blocks = [
        jnp.concatenate([ref[pl.ds(k, DOF, stride=OWN_TILES), :], zero], axis=0)
        for k in range(OWN_TILES)
    ]
    lane = lane_iota()
    tiles = []
    for slot in EDGE_SLOTS:
        first, off = divmod(SET_START[slot], LANES)
        rolled = [pltpu.roll(blocks[first + j], LANES - off, 1) for j in range(3)]
        for j in range(2):
            tiles.append(jnp.where(lane < LANES - off, rolled[j], rolled[j + 1]))
    tiles += blocks[INTERIOR_START // LANES :]
    corner = jnp.zeros((8, LANES), jnp.float32)
    for place, slot in enumerate(CORNER_SLOTS):
        block = blocks[SET_START[slot] // LANES]
        corner = jnp.where(lane // CORNER == place, block, corner)
    tiles.append(corner)
    return tiles


def from_tables(tiles, out_ref):
    lane = lane_iota()
    blocks = [jnp.zeros((8, LANES), jnp.float32) for _ in range(INTERIOR_START // LANES)]
    for e, slot in enumerate(EDGE_SLOTS):
        first, off = divmod(SET_START[slot], LANES)
        rolled = [pltpu.roll(tiles[2 * e + j], off, 1) for j in range(2)]
        blocks[first] = jnp.where(lane >= off, rolled[0], blocks[first])
        blocks[first + 1] = jnp.where(lane >= off, rolled[1], rolled[0])
        blocks[first + 2] = jnp.where(lane < off, rolled[1], blocks[first + 2])
    for place, slot in enumerate(CORNER_SLOTS):
        k = SET_START[slot] // LANES
        blocks[k] = jnp.where(lane // CORNER == place, tiles[CORNER_TILE], blocks[k])
    blocks += tiles[8:CORNER_TILE]
    for k in range(OWN_TILES):
        out_ref[pl.ds(k, DOF, stride=OWN_TILES), :] = blocks[k][:DOF]


def row_of(ref, r):
    return ref[pl.ds(r, 1), :]


def build_onehot(index, onehot_ref):
    rows = index.shape[0]
    lane = (index & (NBND - 1)).astype(jnp.float32).T
    base = lax.broadcasted_iota(jnp.int32, (LANES, NBND), 1).astype(jnp.float32).astype(jnp.bfloat16)
    one, zero = jnp.ones((), jnp.bfloat16), jnp.zeros((), jnp.bfloat16)
    for r in range(rows):
        q = jnp.broadcast_to(lane[:, r : r + 1], (LANES, LANES)).astype(jnp.bfloat16)
        q = jnp.concatenate([q, q], axis=1)
        onehot_ref[r * LANES : (r + 1) * LANES, :] = jnp.where(base == q, one, zero)


def forces(lam, jac_ref, force_ref):
    rows = lam[0].shape[0]
    for d in range(DOF):
        f = jac_ref[d] * lam[0]
        f = f + jac_ref[DOF + d] * lam[1]
        f = f + jac_ref[2 * DOF + d] * lam[2]
        force_ref[d * rows : (d + 1) * rows, :] = f
    for d in range(DOF, 8):
        force_ref[d * rows : (d + 1) * rows, :] = jnp.zeros_like(f)


def spread(force_ref, index_ref, left_ref, heads):
    rows = index_ref.shape[0]
    for r in range(rows):
        f = force_ref[pl.ds(r, 8, stride=rows), :]
        hi = f.astype(jnp.bfloat16).astype(jnp.float32)
        lo = f - hi
        both = jnp.concatenate([hi, lo], axis=0)
        head = jnp.broadcast_to(row_of(index_ref, r) >> 8, (16, LANES))
        for k, h in enumerate(heads):
            left_ref[16 * k : 16 * (k + 1), r * LANES : (r + 1) * LANES] = jnp.where(
                head == h, both, 0.0
            ).astype(jnp.bfloat16)


X_HEADS = (0, 3, 7)
REST_HEADS = (1, 2, 4, 5, 6)


def with_halo(heads):
    return heads + tuple(h + 8 for h in heads if h < 4 or h == 7)


def scatter(lam, jac_a, jac_b, id_a, id_b, hot_a, hot_b, force, left_a, left_b, heads):
    contract = (((1,), (0,)), ((), ()))
    both = with_halo(heads)
    left_a, left_b = left_a.at[: 16 * len(heads)], left_b.at[: 16 * len(both)]
    forces(lam, jac_a, force)
    spread(force, id_a, left_a, heads)
    sum_a = lax.dot_general(left_a[...], hot_a[...], contract, preferred_element_type=jnp.float32)
    forces(lam, jac_b, force)
    spread(force, id_b, left_b, both)
    sum_b = lax.dot_general(left_b[...], hot_b[...], contract, preferred_element_type=jnp.float32)

    def tile(s, k, j):
        lanes = slice(j * LANES, (j + 1) * LANES)
        return s[16 * k : 16 * k + 8, lanes] + s[16 * k + 8 : 16 * k + 16, lanes]

    own, halo = {}, {}
    for k, h in enumerate(both):
        for j in range(2):
            if h < 8:
                own[2 * h + j] = tile(sum_a, k, j) + tile(sum_b, k, j)
            elif h < 12:
                halo[2 * (h - 8) + j] = tile(sum_b, k, j)
    halo_corner = both.index(15) if 15 in both else None
    if halo_corner is not None:
        halo[HALO_CORNER] = tile(sum_b, halo_corner, 1)
    return own, halo


def is_even():
    return lax.rem(lax.axis_index("gy"), 2) == 0


GROUP = 32
LAST_GROUP = 24


def put_edges(even, group, minus, plus, a_ref, b_ref):
    for k, (m, p) in enumerate(zip(minus, plus)):
        rows = slice(group + DOF * k, group + DOF * (k + 1))
        a_ref[rows, :] = jnp.where(even, m[:DOF], p[:DOF])
        b_ref[rows, :] = jnp.where(even, p[:DOF], m[:DOF])


def blocks(tiles):
    block = lane_iota() // CORNER
    out = tiles[3]
    for k in range(3):
        out = jnp.where(block == k, tiles[k], out)
    return out


def put_x(even, groups, a_ref, b_ref):
    size = a_ref.shape[0] // len(groups)
    for g, (first, second) in enumerate(groups):
        up, down = [second[6], second[7]], [second[0], second[1]]
        if first is not None:
            up, down = [first[6], first[7]] + up, [first[0], first[1]] + down
        theirs = second[CORNER_TILE] if CORNER_TILE in second else second[HALO_CORNER]
        ours = jnp.zeros_like(theirs) if first is None else first[CORNER_TILE]
        ours_on, theirs_on = pltpu.roll(ours, CORNER, 1), pltpu.roll(theirs, CORNER, 1)
        theirs_half = pltpu.roll(theirs, 2 * CORNER, 1)
        corner_down = blocks([ours, theirs_on, ours_on, theirs_half])
        corner_up = blocks([ours_on, theirs_half, ours, theirs_on])
        put_edges(even, g * size, down, up, a_ref, b_ref)
        last = slice((g + 1) * size - 8, (g + 1) * size)
        a_ref[last, :] = jnp.where(even, corner_down, corner_up)
        b_ref[last, :] = jnp.where(even, corner_up, corner_down)


class Received:
    def __init__(self, even, a_ref, b_ref, e_ref=None, o_ref=None):
        def pick(when, other):
            def tile(row):
                return jnp.where(even, when[pl.ds(row, 8), :], other[pl.ds(row, 8), :])

            return tile

        self.rows = GROUP if a_ref.shape[0] % GROUP == 0 else LAST_GROUP
        self.x_low, self.x_high = pick(b_ref, a_ref), pick(a_ref, b_ref)
        if e_ref is not None:
            self.y_low, self.y_high = pick(e_ref, o_ref), pick(o_ref, e_ref)

    def edge(self, side, plane):
        place = 2 * (plane % 2) if self.rows == GROUP else 0
        base = self.rows * (plane // 2) + DOF * place
        return [side(base), side(base + DOF)]

    def corner(self, plane):
        odd = (lane_iota() & CORNER) != 0
        row = self.rows * (plane // 2) + self.rows - 8
        low, high = self.y_low(row), self.y_high(row)
        if plane % 2:
            return jnp.where(odd, pltpu.roll(high, 2 * CORNER, 1), pltpu.roll(low, 3 * CORNER, 1))
        return jnp.where(odd, pltpu.roll(high, 3 * CORNER, 1), low)


X_EDGES = (0, 1, 6, 7)
Y_EDGES = (2, 3, 4, 5)
INTERIOR = tuple(range(8, CORNER_TILE))


def x_plane(came, plane):
    low, high = came.edge(came.x_low, plane), came.edge(came.x_high, plane)
    return dict(zip(X_EDGES, low + high))


def y_plane(came, plane):
    low, high = came.edge(came.y_low, plane), came.edge(came.y_high, plane)
    return dict(zip(Y_EDGES, low + high))


def put_dict(ref, tiles):
    for t, value in tiles.items():
        ref[t] = value


def first_kernel(*refs):
    sources, kept, outs = refs[:12], refs[12:20], refs[20:30]
    body_a, body_b, start, minv, force, left_a, left_b, sems = refs[30:]
    id_a, id_b, hot_a, hot_b, own, halo, v_own, m_own, xa, xb = outs
    jac_a, jac_b, precond, bias, mu, stick, act, lam0 = kept
    goals = (body_a, body_b, act, lam0, jac_a, jac_b, start, minv, precond, bias, mu, stick)
    copies = [pltpu.make_async_copy(s, g, sems.at[k]) for k, (s, g) in enumerate(zip(sources, goals))]
    for copy in copies:
        copy.start()
    even = is_even()
    copies[0].wait()
    id_a[...] = table_index(body_a[...])
    build_onehot(id_a[...], hot_a)
    copies[1].wait()
    id_b[...] = table_index(body_b[...])
    build_onehot(id_b[...], hot_b)
    for copy in copies[2:6]:
        copy.wait()
    active = act[...].astype(jnp.float32)
    lam = [active * lam0[k] for k in range(ROWS)]
    for k in range(ROWS):
        lam0[k] = lam[k]
    sums, sums_halo = scatter(lam, jac_a, jac_b, id_a, id_b, hot_a, hot_b, force, left_a, left_b, X_HEADS)
    for copy in copies[6:8]:
        copy.wait()
    v, m = to_tables(start), to_tables(minv)
    for t in range(OWN_TILES):
        v_own[t], m_own[t] = v[t], m[t]
    put_dict(own, sums)
    put_dict(halo, sums_halo)
    put_x(even, [(sums, sums_halo), (dict(enumerate(v)), dict(enumerate(m)))], xa, xb)
    for copy in copies[8:]:
        copy.wait()


def turn_kernel(ra, rb, e_in, o_in, e_ref, o_ref):
    even = is_even()
    came = Received(even, ra, rb)
    left = lane_iota() < 2 * CORNER
    for g in range(0, ra.shape[0], came.rows):
        row = g + came.rows - 8
        low, high = came.x_low(row), came.x_high(row)
        minus, plus = jnp.where(left, high, low), jnp.where(left, low, high)
        e_ref[row : row + 8, :] = jnp.where(even, minus, plus)
        o_ref[row : row + 8, :] = jnp.where(even, plus, minus)


def gather(table, index, codes, start=None):
    values = [[] for _ in range(DOF)]
    for g in range(0, index.shape[0], 8):
        lane = index[g : g + 8] & (LANES - 1)
        code = index[g : g + 8] >> 7
        if start is None:
            part = [jnp.zeros(lane.shape, jnp.float32) for _ in range(DOF)]
        else:
            part = [start[d, g : g + 8, :] for d in range(DOF)]
        for c, t in codes:
            mask = code == c
            for d in range(DOF):
                row = jnp.broadcast_to(table[t, d : d + 1, :], lane.shape)
                got = jnp.take_along_axis(row, lane, axis=1, mode="promise_in_bounds")
                part[d] = jnp.where(mask, got, part[d])
        for d in range(DOF):
            values[d].append(part[d])
    return [jnp.concatenate(v, axis=0) for v in values]


def own_codes(tiles):
    return tuple((t, t) for t in tiles)


def halo_codes(tiles):
    return tuple((OWN_TILES + (15 if t == HALO_CORNER else t), OWN_TILES + t) for t in tiles)


def gather_both(table, id_a, id_b, own_tiles, halo_tiles, out, start):
    part = (None, None) if start is None else (start.at[:DOF], start.at[DOF:])
    for ref, ids, codes, first, base in (
        (out, id_a, own_codes(own_tiles), part[0], 0),
        (out, id_b, own_codes(own_tiles) + halo_codes(halo_tiles), part[1], DOF),
    ):
        for d, value in enumerate(gather(table, ids[...], codes, first)):
            ref[base + d] = value


def window_kernel(first, last, jac_a, jac_b, lam, id_a, id_b, hot_a, hot_b, v_own, m_own, own_x, *refs):
    own, e_ref, o_ref, out = refs[:4]
    halo, work = (None, refs[4:]) if last else (refs[4], refs[5:])
    force, left_a, left_b, table, *sem = work
    if last:
        copy = pltpu.make_async_copy(lam, out, sem[0])
        copy.start()
    even = is_even()
    values = [lam[k] for k in range(ROWS)]
    sums, sums_halo = scatter(values, jac_a, jac_b, id_a, id_b, hot_a, hot_b, force, left_a, left_b, REST_HEADS)
    put_dict(own, sums)
    if not last:
        put_dict(halo, sums_halo)
    planes = [(sums_halo,)] if last else [(sums, sums_halo)] + [(v_own, m_own)] * first
    size = e_ref.shape[0] // len(planes)
    for g, pair in enumerate(planes):
        minus = [p[t] for p in pair for t in (2, 3)]
        plus = [p[t] for p in pair for t in (4, 5)]
        put_edges(even, g * size, minus, plus, e_ref, o_ref)
    if last:
        copy.wait()
        return
    for t in INTERIOR:
        table[t] = v_own[t] + m_own[t] * (sums[t] if t in sums else own_x[t])
    gather_both(table, id_a, id_b, INTERIOR, (), out, None)


def side_kernel(first, own, halo, v_own, m_own, id_a, id_b, part, ra, rb, *refs):
    v_halo, m_halo, (out, table) = (None, None, refs) if first else (refs[0], refs[1], refs[2:])
    came = Received(is_even(), ra, rb)
    theirs, ours = x_plane(came, 0), x_plane(came, 1)
    if first:
        v_halo, m_halo = x_plane(came, 2), x_plane(came, 3)
    for t in X_EDGES:
        table[t] = v_own[t] + m_own[t] * (own[t] + ours[t])
        table[OWN_TILES + t] = v_halo[t] + m_halo[t] * (halo[t] + theirs[t])
    gather_both(table, id_a, id_b, X_EDGES, X_EDGES, out, part)


def relative(jac, values):
    out = []
    for k in range(ROWS):
        u = jac[k * DOF] * values[0]
        for d in range(1, DOF):
            u = u + jac[k * DOF + d] * values[d]
        out.append(u)
    return out


def middle_kernel(
    first, last, jac_a, jac_b, precond, bias, mu, stick, act, lam_in,
    id_a, id_b, hot_a, hot_b, own_x, halo_x, own, halo, v_own, m_own, part, ra, rb, qe, qo, *refs,
):
    if not first:
        v_halo, m_halo, *refs = refs
    lam_out, own_out, xa, xb, *made = refs[:-4]
    table, force, left_a, left_b = refs[-4:]
    if first:
        v_halo, m_halo = made[1:]
    even = is_even()
    came = Received(even, ra, rb, qe, qo)
    if first:
        for ref, p in ((v_halo, 2), (m_halo, 3)):
            for t, value in (x_plane(came, p) | y_plane(came, p)).items():
                ref[t] = value
            ref[HALO_CORNER] = came.corner(p)
    theirs, ours = y_plane(came, 0), y_plane(came, 1)
    theirs[HALO_CORNER], ours[CORNER_TILE] = came.corner(0), came.corner(1)
    for t, value in ours.items():
        mine = own_x if t == CORNER_TILE else own
        table[t] = v_own[t] + m_own[t] * (mine[t] + value)
    for t, value in theirs.items():
        mine = halo_x if t == HALO_CORNER else halo
        table[OWN_TILES + t] = v_halo[t] + m_halo[t] * (mine[t] + value)
    late, late_halo = own_codes(ours), halo_codes(theirs)
    v_a = gather(table, id_a[...], late, part.at[:DOF])
    v_b = gather(table, id_b[...], late + late_halo, part.at[DOF:])
    u_a = relative(jac_a, v_a)
    u_b = relative(jac_b, v_b)
    target = [u_a[k] + u_b[k] + bias[k] for k in range(ROWS)]
    active = act[...].astype(jnp.float32)
    lam = [lam_in[k] for k in range(ROWS)]
    raw = []
    for k in range(ROWS):
        w = precond[k * ROWS] * target[0]
        for j in range(1, ROWS):
            w = w + precond[k * ROWS + j] * target[j]
        raw.append(lam[k] - w)
    normal = jnp.maximum(raw[0], 0.0)
    bound = mu[...] * (1.0 + 0.5 * stick[...].astype(jnp.float32)) * normal + 0.1
    square = raw[1] * raw[1] + raw[2] * raw[2]
    scale = bound / jnp.sqrt(jnp.maximum(square, bound * bound))
    lam = [active * normal, active * (raw[1] * scale), active * (raw[2] * scale)]
    for k in range(ROWS):
        lam_out[k] = lam[k]
    sums, sums_halo = scatter(lam, jac_a, jac_b, id_a, id_b, hot_a, hot_b, force, left_a, left_b, X_HEADS)
    put_dict(own_out, sums)
    if not last:
        put_dict(made[0], sums_halo)
    put_x(even, [(None if last else sums, sums_halo)], xa, xb)


def last_kernel(own_x, own, v_own, m_own, ra, rb, qe, qo, out):
    came = Received(is_even(), ra, rb, qe, qo)
    ours = x_plane(came, 1) | y_plane(came, 1)
    ours[CORNER_TILE] = came.corner(1)
    mine = [(own_x if t // 2 in X_HEADS else own)[t] for t in range(OWN_TILES)]
    total = [mine[t] + ours[t] if t in ours else mine[t] for t in range(OWN_TILES)]
    from_tables([v_own[t] + m_own[t] * total[t] for t in range(OWN_TILES)], out)


def exchange_pairs(nx, ny):
    up = []
    for x in range(nx):
        for y in range(ny):
            to = x + 1 if y % 2 == 1 else x - 1
            goal = (to, y) if 0 <= to < nx else (x, y ^ 1)
            up.append((x * ny + y, goal[0] * ny + goal[1]))
    down = [(b, a) for a, b in up]
    near = [(y, y ^ 1) for y in range(ny)]
    far = [(y, (((y + 1) ^ 1) - 1) % ny) for y in range(ny)]
    return up, down, near, far


def on_device(
    velocity0, inv_mass, jac_a, jac_b, precond, bias, friction, impulse0, body_a, body_b, active, sticking
):
    nx, ny = lax.axis_size("gx"), lax.axis_size("gy")
    up, down, near, far = exchange_pairs(nx, ny)
    rows, lanes = body_a.shape[-2:]
    flat = lambda a: a.reshape(-1, rows, lanes)
    plain = lambda a: a.reshape(rows, lanes)
    jac_a, jac_b, precond, bias, impulse0 = map(flat, (jac_a, jac_b, precond, bias, impulse0))
    friction, body_a, body_b, active, sticking = map(plain, (friction, body_a, body_b, active, sticking))
    start, minv = (a.reshape(-1, lanes) for a in (velocity0, inv_mass))
    contacts = rows * lanes
    f32, i32, bf16 = jnp.float32, jnp.int32, jnp.bfloat16
    arr = jax.ShapeDtypeStruct
    vmem = pl.BlockSpec(memory_space=pltpu.VMEM)
    own_t, halo_t = arr((OWN_TILES, 8, lanes), f32), arr((HALO_TILES, 8, lanes), f32)
    lam_t = arr((ROWS, rows, lanes), f32)
    ids_t, hot_t = arr((rows, lanes), i32), arr((contacts, NBND), bf16)
    message = lambda r: arr((r, lanes), f32)
    work = [
        pltpu.VMEM((8 * rows, lanes), f32),
        pltpu.VMEM((16 * len(REST_HEADS), contacts), bf16),
        pltpu.VMEM((16 * len(with_halo(REST_HEADS)), contacts), bf16),
    ]
    table = [pltpu.VMEM((OWN_TILES + HALO_TILES, 8, lanes), f32)]

    def call(kernel, outs, scratch, name, *operands, space=pltpu.VMEM, out_spaces=None, aliases={}, flops=0):
        spaces = out_spaces or jax.tree.map(lambda _: pltpu.VMEM, outs)
        return pl.pallas_call(
            kernel,
            out_shape=outs,
            in_specs=[pl.BlockSpec(memory_space=space)] * len(operands),
            out_specs=jax.tree.map(lambda m: pl.BlockSpec(memory_space=m), spaces),
            scratch_shapes=scratch,
            input_output_aliases=aliases,
            compiler_params=pltpu.CompilerParams(vmem_limit_bytes=32 * 1024 * 1024),
            cost_estimate=pl.CostEstimate(flops=flops, bytes_accessed=0, transcendentals=0) if flops else None,
            name=name,
        )(*operands)

    def along_x(xa, xb):
        return lax.ppermute(xa, ("gx", "gy"), up), lax.ppermute(xb, ("gx", "gy"), down)

    def along_y(ra, rb, ye, yo):
        like = arr(ye.shape, f32)
        ye, yo = call(turn_kernel, (like, like), [], "turn", ra, rb, ye, yo, aliases={2: 0, 3: 1})
        return lax.ppermute(ye, "gy", far), lax.ppermute(yo, "gy", near)

    sources = (body_a, body_b, active, impulse0, jac_a, jac_b, start, minv, precond, bias, friction, sticking)
    like = lambda a: arr(a.shape, a.dtype)
    kept = (jac_a, jac_b, precond, bias, friction, sticking, active, impulse0)
    sources = [pltpu.with_memory_space_constraint(a, pltpu.HBM) for a in sources]
    made = call(
        first_kernel,
        (*map(like, kept), ids_t, ids_t, hot_t, hot_t, own_t, halo_t, own_t, own_t, message(2 * GROUP), message(2 * GROUP)),
        [pltpu.VMEM(a.shape, a.dtype) for a in (body_a, body_b, start, minv)]
        + work
        + [pltpu.SemaphoreType.DMA((len(sources),))],
        "first",
        *sources,
        space=pltpu.HBM,
    )
    fixed, lam = made[:7], made[7]
    id_a, id_b, hot_a, hot_b, own_x, halo_x, v_own, m_own, xa, xb = made[8:]
    part_t = arr((2 * DOF, rows, lanes), f32)
    halo_tables = ()
    ids = (id_a, id_b)
    hots = (hot_a, hot_b)
    for step in range(ITERS):
        first, last = step == 0, step == ITERS - 1
        came_x = along_x(xa, xb)
        sent = message(GROUP * (2 if first else 1))
        own, ye, yo, part, halo = call(
            lambda *refs, first=first: window_kernel(first, False, *refs),
            (own_t, sent, sent, part_t, halo_t), work + table, "window",
            *fixed[:2], lam, *ids, *hots, v_own, m_own, own_x,
        )
        came_y = along_y(*came_x, ye, yo)
        part = call(
            lambda *refs, first=first: side_kernel(first, *refs), part_t, table, "side",
            own_x, halo_x, v_own, m_own, *ids, part, *came_x, *halo_tables,
        )
        sent = message(LAST_GROUP if last else GROUP)
        outs = (lam_t, own_t, sent, sent) + (halo_t,) * (3 if first else 0 if last else 1)
        lam, own_x, xa, xb, *made = call(
            lambda *refs, first=first, last=last: middle_kernel(first, last, *refs), outs, table + work, "middle",
            *fixed, lam, *ids, *hots, own_x, halo_x, own, halo, v_own, m_own, part, *came_x, *came_y, *halo_tables,
        )
        if not last:
            halo_x = made[0]
        if first:
            halo_tables = tuple(made[1:])
    came_x = along_x(xa, xb)
    own, ye, yo, lam = call(
        lambda *refs: window_kernel(False, True, *refs),
        (own_t, sent, sent, lam_t), work + table + [pltpu.SemaphoreType.DMA], "window",
        *fixed[:2], lam, *ids, *hots, v_own, m_own, own_x,
        out_spaces=(pltpu.VMEM,) * 3 + (pltpu.HBM,),
    )
    came_y = along_y(*came_x, ye, yo)
    out = call(last_kernel, arr(start.shape, f32), [], "last", own_x, own, v_own, m_own, *came_x, *came_y)
    return lam.reshape(ROWS, 1, 1, rows, lanes), out.reshape(velocity0.shape)


def solution(mesh):
    whole = ("groups", "gx")
    body = P(None, whole, "gy", None)
    many = P(None, whole, "gy", None, None)
    one = P(whole, "gy", None, None)
    return jax.shard_map(
        on_device,
        mesh=mesh,
        in_specs=(body, body, many, many, many, many, one, many, one, one, one, one),
        out_specs=(many, body),
        check_vma=False,
    )
```

```python
import jax
import jax.numpy as jnp
import numpy as np
from jax import lax
from jax.experimental import pallas as pl
from jax.experimental.pallas import tpu as pltpu
from jax.sharding import PartitionSpec as P

ROWS = 3
DOF = 6
ITERS = 3
LANES = 128
NB = 2048
NBND = 256
CORNER = NBND // 8
OWN_TILES = NB // LANES
EDGE_TILES = 2
HALO_TILES = 9
CORNER_TILE = OWN_TILES - 1
HALO_CORNER = HALO_TILES - 1
SET_START = (0, 32, 288, 320, 576, 832, 864, 1120)
TABLE_START = (1920, 0, 1952, 256, 512, 1984, 768, 2016)
INTERIOR_START = 1152
INTERIOR_TABLE = 1024
EDGE_SLOTS = (1, 3, 4, 6)
CORNER_SLOTS = (0, 2, 5, 7)


def table_index(body):
    steps = []
    for slot in range(8):
        steps.append((SET_START[slot], TABLE_START[slot] - SET_START[slot]))
    steps.append((INTERIOR_START, INTERIOR_TABLE - INTERIOR_START))
    for slot in range(8):
        steps.append((NB + slot * NBND, TABLE_START[slot] - slot * NBND))
    shift = jnp.full(body.shape, steps[0][1], jnp.int32)
    for start, delta in steps[1:]:
        shift = jnp.where(body >= start, delta, shift)
    return body + shift


def lane_iota():
    return lax.broadcasted_iota(jnp.int32, (8, LANES), 1)


def to_tables(ref):
    zero = jnp.zeros((2, LANES), jnp.float32)
    blocks = [
        jnp.concatenate([ref[pl.ds(k, DOF, stride=OWN_TILES), :], zero], axis=0)
        for k in range(OWN_TILES)
    ]
    lane = lane_iota()
    tiles = []
    for slot in EDGE_SLOTS:
        first, off = divmod(SET_START[slot], LANES)
        rolled = [pltpu.roll(blocks[first + j], LANES - off, 1) for j in range(3)]
        for j in range(2):
            tiles.append(jnp.where(lane < LANES - off, rolled[j], rolled[j + 1]))
    tiles += blocks[INTERIOR_START // LANES :]
    corner = jnp.zeros((8, LANES), jnp.float32)
    for place, slot in enumerate(CORNER_SLOTS):
        block = blocks[SET_START[slot] // LANES]
        corner = jnp.where(lane // CORNER == place, block, corner)
    tiles.append(corner)
    return tiles


def from_tables(tiles, out_ref):
    lane = lane_iota()
    blocks = [jnp.zeros((8, LANES), jnp.float32) for _ in range(INTERIOR_START // LANES)]
    for e, slot in enumerate(EDGE_SLOTS):
        first, off = divmod(SET_START[slot], LANES)
        rolled = [pltpu.roll(tiles[2 * e + j], off, 1) for j in range(2)]
        blocks[first] = jnp.where(lane >= off, rolled[0], blocks[first])
        blocks[first + 1] = jnp.where(lane >= off, rolled[1], rolled[0])
        blocks[first + 2] = jnp.where(lane < off, rolled[1], blocks[first + 2])
    for place, slot in enumerate(CORNER_SLOTS):
        k = SET_START[slot] // LANES
        blocks[k] = jnp.where(lane // CORNER == place, tiles[CORNER_TILE], blocks[k])
    blocks += tiles[8:CORNER_TILE]
    for k in range(OWN_TILES):
        out_ref[pl.ds(k, DOF, stride=OWN_TILES), :] = blocks[k][:DOF]


def row_of(ref, r):
    return ref[pl.ds(r, 1), :]


def build_onehot(index, onehot_ref):
    rows = index.shape[0]
    lane = (index & (NBND - 1)).astype(jnp.float32).T
    base = lax.broadcasted_iota(jnp.int32, (LANES, NBND), 1).astype(jnp.float32).astype(jnp.bfloat16)
    one, zero = jnp.ones((), jnp.bfloat16), jnp.zeros((), jnp.bfloat16)
    for r in range(rows):
        q = jnp.broadcast_to(lane[:, r : r + 1], (LANES, LANES)).astype(jnp.bfloat16)
        q = jnp.concatenate([q, q], axis=1)
        onehot_ref[r * LANES : (r + 1) * LANES, :] = jnp.where(base == q, one, zero)


def forces(lam, jac_ref, force_ref):
    rows = lam[0].shape[0]
    for d in range(DOF):
        f = jac_ref[d] * lam[0]
        f = f + jac_ref[DOF + d] * lam[1]
        f = f + jac_ref[2 * DOF + d] * lam[2]
        force_ref[d * rows : (d + 1) * rows, :] = f
    for d in range(DOF, 8):
        force_ref[d * rows : (d + 1) * rows, :] = jnp.zeros_like(f)


def spread(force_ref, index_ref, left_ref, heads):
    rows = index_ref.shape[0]
    for r in range(rows):
        f = force_ref[pl.ds(r, 8, stride=rows), :]
        hi = f.astype(jnp.bfloat16).astype(jnp.float32)
        lo = f - hi
        head = jnp.broadcast_to(row_of(index_ref, r) >> 8, (8, LANES))
        for k, h in enumerate(heads):
            mask = head == h
            both = jnp.concatenate([jnp.where(mask, hi, 0.0), jnp.where(mask, lo, 0.0)], axis=0)
            left_ref[16 * k : 16 * (k + 1), r * LANES : (r + 1) * LANES] = both.astype(jnp.bfloat16)


X_HEADS = (0, 3, 7)
REST_HEADS = (1, 2, 4, 5, 6)


def with_halo(heads):
    return heads + tuple(h + 8 for h in heads if h < 4 or h == 7)


def scatter(lam, jac_a, jac_b, id_a, id_b, hot, force, left, heads, between=None):
    contacts = hot.shape[0] // 2
    both = with_halo(heads)
    rows, own_rows = 16 * len(both), 16 * len(heads)
    forces(lam, jac_a, force)
    spread(force, id_a, left.at[:own_rows, :contacts], heads)
    left[own_rows:rows, :contacts] = jnp.zeros((rows - own_rows, contacts), jnp.bfloat16)
    if between is not None:
        sums = jnp.dot(left[:rows, :contacts], hot[:contacts, :], preferred_element_type=jnp.float32)
        between()
    forces(lam, jac_b, force)
    spread(force, id_b, left.at[:rows, contacts:], both)
    if between is None:
        sums = jnp.dot(left[:rows, :], hot[...], preferred_element_type=jnp.float32)
    else:
        sums = sums + jnp.dot(left[:rows, contacts:], hot[contacts:, :], preferred_element_type=jnp.float32)

    def tile(k, j):
        lanes = slice(j * LANES, (j + 1) * LANES)
        return sums[16 * k : 16 * k + 8, lanes] + sums[16 * k + 8 : 16 * k + 16, lanes]

    own, halo = {}, {}
    for k, h in enumerate(both):
        for j in range(2):
            if h < 8:
                own[2 * h + j] = tile(k, j)
            elif h < 12:
                halo[2 * (h - 8) + j] = tile(k, j)
    if 15 in both:
        halo[HALO_CORNER] = tile(both.index(15), 1)
    return own, halo


def is_even():
    return lax.rem(lax.axis_index("gy"), 2) == 0


GROUP = 32
LAST_GROUP = 24


def put_edges(even, group, minus, plus, a_ref, b_ref):
    for k, (m, p) in enumerate(zip(minus, plus)):
        rows = slice(group + DOF * k, group + DOF * (k + 1))
        a_ref[rows, :] = jnp.where(even, m[:DOF], p[:DOF])
        b_ref[rows, :] = jnp.where(even, p[:DOF], m[:DOF])


def blocks(tiles):
    block = lane_iota() // CORNER
    out = tiles[3]
    for k in range(3):
        out = jnp.where(block == k, tiles[k], out)
    return out


def put_x(even, groups, a_ref, b_ref):
    size = a_ref.shape[0] // len(groups)
    for g, (first, second) in enumerate(groups):
        up, down = [second[6], second[7]], [second[0], second[1]]
        if first is not None:
            up, down = [first[6], first[7]] + up, [first[0], first[1]] + down
        theirs = second[CORNER_TILE] if CORNER_TILE in second else second[HALO_CORNER]
        ours = jnp.zeros_like(theirs) if first is None else first[CORNER_TILE]
        ours_on, theirs_on = pltpu.roll(ours, CORNER, 1), pltpu.roll(theirs, CORNER, 1)
        theirs_half = pltpu.roll(theirs, 2 * CORNER, 1)
        corner_down = blocks([ours, theirs_on, ours_on, theirs_half])
        corner_up = blocks([ours_on, theirs_half, ours, theirs_on])
        put_edges(even, g * size, down, up, a_ref, b_ref)
        last = slice((g + 1) * size - 8, (g + 1) * size)
        a_ref[last, :] = jnp.where(even, corner_down, corner_up)
        b_ref[last, :] = jnp.where(even, corner_up, corner_down)


class Received:
    def __init__(self, even, a_ref, b_ref, e_ref=None, o_ref=None):
        def pick(when, other):
            def tile(row):
                return jnp.where(even, when[pl.ds(row, 8), :], other[pl.ds(row, 8), :])

            return tile

        self.rows = GROUP if a_ref.shape[0] % GROUP == 0 else LAST_GROUP
        self.x_low, self.x_high = pick(b_ref, a_ref), pick(a_ref, b_ref)
        if e_ref is not None:
            self.y_low, self.y_high = pick(e_ref, o_ref), pick(o_ref, e_ref)

    def edge(self, side, plane):
        place = 2 * (plane % 2) if self.rows == GROUP else 0
        base = self.rows * (plane // 2) + DOF * place
        return [side(base), side(base + DOF)]

    def corner(self, plane):
        odd = (lane_iota() & CORNER) != 0
        row = self.rows * (plane // 2) + self.rows - 8
        low, high = self.y_low(row), self.y_high(row)
        if plane % 2:
            return jnp.where(odd, pltpu.roll(high, 2 * CORNER, 1), pltpu.roll(low, 3 * CORNER, 1))
        return jnp.where(odd, pltpu.roll(high, 3 * CORNER, 1), low)


X_EDGES = (0, 1, 6, 7)
Y_EDGES = (2, 3, 4, 5)
INTERIOR = tuple(range(8, CORNER_TILE))


def x_plane(came, plane):
    low, high = came.edge(came.x_low, plane), came.edge(came.x_high, plane)
    return dict(zip(X_EDGES, low + high))


def y_plane(came, plane):
    low, high = came.edge(came.y_low, plane), came.edge(came.y_high, plane)
    return dict(zip(Y_EDGES, low + high))


def put_dict(ref, tiles):
    for t, value in tiles.items():
        ref[t] = value


def first_kernel(*refs):
    sources, kept, outs = refs[:12], refs[12:20], refs[20:29]
    body_a, body_b, start, minv, force, left, sems = refs[29:]
    id_a, id_b, hot, own, halo, v_own, m_own, xa, xb = outs
    jac_a, jac_b, precond, bias, mu, stick, act, lam0 = kept
    goals = (body_a, body_b, act, lam0, jac_a, jac_b, start, minv, precond, bias, mu, stick)
    copies = [pltpu.make_async_copy(s, g, sems.at[k]) for k, (s, g) in enumerate(zip(sources, goals))]
    for copy in copies:
        copy.start()
    even = is_even()
    copies[0].wait()
    id_a[...] = table_index(body_a[...])
    build_onehot(id_a[...], hot.at[: hot.shape[0] // 2])
    copies[1].wait()
    id_b[...] = table_index(body_b[...])
    for copy in copies[2:6]:
        copy.wait()
    active = act[...].astype(jnp.float32)
    lam = [active * lam0[k] for k in range(ROWS)]
    for k in range(ROWS):
        lam0[k] = lam[k]
    sums, sums_halo = scatter(
        lam, jac_a, jac_b, id_a, id_b, hot, force, left, X_HEADS,
        between=lambda: build_onehot(id_b[...], hot.at[hot.shape[0] // 2 :]),
    )
    for copy in copies[6:8]:
        copy.wait()
    v, m = to_tables(start), to_tables(minv)
    for t in range(OWN_TILES):
        v_own[t], m_own[t] = v[t], m[t]
    put_dict(own, sums)
    put_dict(halo, sums_halo)
    put_x(even, [(sums, sums_halo), (dict(enumerate(v)), dict(enumerate(m)))], xa, xb)
    for copy in copies[8:]:
        copy.wait()


def turn_kernel(ra, rb, e_in, o_in, e_ref, o_ref):
    even = is_even()
    came = Received(even, ra, rb)
    left = lane_iota() < 2 * CORNER
    for g in range(0, ra.shape[0], came.rows):
        row = g + came.rows - 8
        low, high = came.x_low(row), came.x_high(row)
        minus, plus = jnp.where(left, high, low), jnp.where(left, low, high)
        e_ref[row : row + 8, :] = jnp.where(even, minus, plus)
        o_ref[row : row + 8, :] = jnp.where(even, plus, minus)


def gather(table, index, codes, start=None):
    values = [[] for _ in range(DOF)]
    for g in range(0, index.shape[0], 8):
        lane = index[g : g + 8] & (LANES - 1)
        code = index[g : g + 8] >> 7
        if start is None:
            part = [jnp.zeros(lane.shape, jnp.float32) for _ in range(DOF)]
        else:
            part = [start[d, g : g + 8, :] for d in range(DOF)]
        for c, t in codes:
            mask = code == c
            for d in range(DOF):
                row = jnp.broadcast_to(table[t, d : d + 1, :], lane.shape)
                got = jnp.take_along_axis(row, lane, axis=1, mode="promise_in_bounds")
                part[d] = jnp.where(mask, got, part[d])
        for d in range(DOF):
            values[d].append(part[d])
    return [jnp.concatenate(v, axis=0) for v in values]


def own_codes(tiles):
    return tuple((t, t) for t in tiles)


def halo_codes(tiles):
    return tuple((OWN_TILES + (15 if t == HALO_CORNER else t), OWN_TILES + t) for t in tiles)


def gather_both(table, id_a, id_b, own_tiles, halo_tiles, out, start):
    part = (None, None) if start is None else (start.at[:DOF], start.at[DOF:])
    for ref, ids, codes, first, base in (
        (out, id_a, own_codes(own_tiles), part[0], 0),
        (out, id_b, own_codes(own_tiles) + halo_codes(halo_tiles), part[1], DOF),
    ):
        for d, value in enumerate(gather(table, ids[...], codes, first)):
            ref[base + d] = value


def window_kernel(first, last, jac_a, jac_b, lam, id_a, id_b, hot, v_own, m_own, own_x, *refs):
    own, e_ref, o_ref, out = refs[:4]
    halo, work = (None, refs[4:]) if last else (refs[4], refs[5:])
    force, left, table, *sem = work
    if last:
        copy = pltpu.make_async_copy(lam, out, sem[0])
        copy.start()
    even = is_even()
    values = [lam[k] for k in range(ROWS)]
    sums, sums_halo = scatter(values, jac_a, jac_b, id_a, id_b, hot, force, left, REST_HEADS)
    put_dict(own, sums)
    if not last:
        put_dict(halo, sums_halo)
    planes = [(sums_halo,)] if last else [(sums, sums_halo)] + [(v_own, m_own)] * first
    size = e_ref.shape[0] // len(planes)
    for g, pair in enumerate(planes):
        minus = [p[t] for p in pair for t in (2, 3)]
        plus = [p[t] for p in pair for t in (4, 5)]
        put_edges(even, g * size, minus, plus, e_ref, o_ref)
    if last:
        copy.wait()
        return
    for t in INTERIOR:
        table[t] = v_own[t] + m_own[t] * (sums[t] if t in sums else own_x[t])
    gather_both(table, id_a, id_b, INTERIOR, (), out, None)


def side_kernel(first, own, halo, v_own, m_own, id_a, id_b, part, ra, rb, *refs):
    v_halo, m_halo, (out, table) = (None, None, refs) if first else (refs[0], refs[1], refs[2:])
    came = Received(is_even(), ra, rb)
    theirs, ours = x_plane(came, 0), x_plane(came, 1)
    if first:
        v_halo, m_halo = x_plane(came, 2), x_plane(came, 3)
    for t in X_EDGES:
        table[t] = v_own[t] + m_own[t] * (own[t] + ours[t])
        table[OWN_TILES + t] = v_halo[t] + m_halo[t] * (halo[t] + theirs[t])
    gather_both(table, id_a, id_b, X_EDGES, X_EDGES, out, part)


def relative(jac, values):
    out = []
    for k in range(ROWS):
        u = jac[k * DOF] * values[0]
        for d in range(1, DOF):
            u = u + jac[k * DOF + d] * values[d]
        out.append(u)
    return out


def middle_kernel(
    first, last, jac_a, jac_b, precond, bias, mu, stick, act, lam_in,
    id_a, id_b, hot, own_x, halo_x, own, halo, v_own, m_own, part, ra, rb, qe, qo, *refs,
):
    if not first:
        v_halo, m_halo, *refs = refs
    lam_out, own_out, xa, xb, *made = refs[:-3]
    table, force, left = refs[-3:]
    if first:
        v_halo, m_halo = made[1:]
    even = is_even()
    came = Received(even, ra, rb, qe, qo)
    if first:
        for ref, p in ((v_halo, 2), (m_halo, 3)):
            for t, value in (x_plane(came, p) | y_plane(came, p)).items():
                ref[t] = value
            ref[HALO_CORNER] = came.corner(p)
    theirs, ours = y_plane(came, 0), y_plane(came, 1)
    theirs[HALO_CORNER], ours[CORNER_TILE] = came.corner(0), came.corner(1)
    for t, value in ours.items():
        mine = own_x if t == CORNER_TILE else own
        table[t] = v_own[t] + m_own[t] * (mine[t] + value)
    for t, value in theirs.items():
        mine = halo_x if t == HALO_CORNER else halo
        table[OWN_TILES + t] = v_halo[t] + m_halo[t] * (mine[t] + value)
    late, late_halo = own_codes(ours), halo_codes(theirs)
    v_a = gather(table, id_a[...], late, part.at[:DOF])
    v_b = gather(table, id_b[...], late + late_halo, part.at[DOF:])
    u_a = relative(jac_a, v_a)
    u_b = relative(jac_b, v_b)
    target = [u_a[k] + u_b[k] + bias[k] for k in range(ROWS)]
    active = act[...].astype(jnp.float32)
    lam = [lam_in[k] for k in range(ROWS)]
    raw = []
    for k in range(ROWS):
        w = precond[k * ROWS] * target[0]
        for j in range(1, ROWS):
            w = w + precond[k * ROWS + j] * target[j]
        raw.append(lam[k] - w)
    normal = jnp.maximum(raw[0], 0.0)
    bound = mu[...] * (1.0 + 0.5 * stick[...].astype(jnp.float32)) * normal + 0.1
    square = raw[1] * raw[1] + raw[2] * raw[2]
    scale = bound / jnp.sqrt(jnp.maximum(square, bound * bound))
    lam = [active * normal, active * (raw[1] * scale), active * (raw[2] * scale)]
    for k in range(ROWS):
        lam_out[k] = lam[k]
    sums, sums_halo = scatter(lam, jac_a, jac_b, id_a, id_b, hot, force, left, X_HEADS)
    put_dict(own_out, sums)
    if not last:
        put_dict(made[0], sums_halo)
    put_x(even, [(None if last else sums, sums_halo)], xa, xb)


def last_kernel(own_x, own, v_own, m_own, ra, rb, qe, qo, out):
    came = Received(is_even(), ra, rb, qe, qo)
    ours = x_plane(came, 1) | y_plane(came, 1)
    ours[CORNER_TILE] = came.corner(1)
    mine = [(own_x if t // 2 in X_HEADS else own)[t] for t in range(OWN_TILES)]
    total = [mine[t] + ours[t] if t in ours else mine[t] for t in range(OWN_TILES)]
    from_tables([v_own[t] + m_own[t] * total[t] for t in range(OWN_TILES)], out)


def exchange_pairs(nx, ny):
    up = []
    for x in range(nx):
        for y in range(ny):
            to = x + 1 if y % 2 == 1 else x - 1
            goal = (to, y) if 0 <= to < nx else (x, y ^ 1)
            up.append((x * ny + y, goal[0] * ny + goal[1]))
    down = [(b, a) for a, b in up]
    near = [(y, y ^ 1) for y in range(ny)]
    far = [(y, (((y + 1) ^ 1) - 1) % ny) for y in range(ny)]
    return up, down, near, far


def on_device(
    velocity0, inv_mass, jac_a, jac_b, precond, bias, friction, impulse0, body_a, body_b, active, sticking
):
    nx, ny = lax.axis_size("gx"), lax.axis_size("gy")
    up, down, near, far = exchange_pairs(nx, ny)
    rows, lanes = body_a.shape[-2:]
    flat = lambda a: a.reshape(-1, rows, lanes)
    plain = lambda a: a.reshape(rows, lanes)
    jac_a, jac_b, precond, bias, impulse0 = map(flat, (jac_a, jac_b, precond, bias, impulse0))
    friction, body_a, body_b, active, sticking = map(plain, (friction, body_a, body_b, active, sticking))
    start, minv = (a.reshape(-1, lanes) for a in (velocity0, inv_mass))
    contacts = rows * lanes
    f32, i32, bf16 = jnp.float32, jnp.int32, jnp.bfloat16
    arr = jax.ShapeDtypeStruct
    vmem = pl.BlockSpec(memory_space=pltpu.VMEM)
    own_t, halo_t = arr((OWN_TILES, 8, lanes), f32), arr((HALO_TILES, 8, lanes), f32)
    lam_t = arr((ROWS, rows, lanes), f32)
    ids_t, hot_t = arr((rows, lanes), i32), arr((2 * contacts, NBND), bf16)
    message = lambda r: arr((r, lanes), f32)
    work = [
        pltpu.VMEM((8 * rows, lanes), f32),
        pltpu.VMEM((16 * len(with_halo(REST_HEADS)), 2 * contacts), bf16),
    ]
    table = [pltpu.VMEM((OWN_TILES + HALO_TILES, 8, lanes), f32)]

    def call(kernel, outs, scratch, name, *operands, space=pltpu.VMEM, out_spaces=None, aliases={}, flops=0):
        spaces = out_spaces or jax.tree.map(lambda _: pltpu.VMEM, outs)
        return pl.pallas_call(
            kernel,
            out_shape=outs,
            in_specs=[pl.BlockSpec(memory_space=space)] * len(operands),
            out_specs=jax.tree.map(lambda m: pl.BlockSpec(memory_space=m), spaces),
            scratch_shapes=scratch,
            input_output_aliases=aliases,
            compiler_params=pltpu.CompilerParams(vmem_limit_bytes=32 * 1024 * 1024),
            cost_estimate=pl.CostEstimate(flops=flops, bytes_accessed=0, transcendentals=0) if flops else None,
            name=name,
        )(*operands)

    def along_x(xa, xb):
        return lax.ppermute(xa, ("gx", "gy"), up), lax.ppermute(xb, ("gx", "gy"), down)

    def along_y(ra, rb, ye, yo):
        like = arr(ye.shape, f32)
        ye, yo = call(turn_kernel, (like, like), [], "turn", ra, rb, ye, yo, aliases={2: 0, 3: 1})
        return lax.ppermute(ye, "gy", far), lax.ppermute(yo, "gy", near)

    sources = (body_a, body_b, active, impulse0, jac_a, jac_b, start, minv, precond, bias, friction, sticking)
    like = lambda a: arr(a.shape, a.dtype)
    kept = (jac_a, jac_b, precond, bias, friction, sticking, active, impulse0)
    sources = [pltpu.with_memory_space_constraint(a, pltpu.HBM) for a in sources]
    made = call(
        first_kernel,
        (*map(like, kept), ids_t, ids_t, hot_t, own_t, halo_t, own_t, own_t, message(2 * GROUP), message(2 * GROUP)),
        [pltpu.VMEM(a.shape, a.dtype) for a in (body_a, body_b, start, minv)]
        + work
        + [pltpu.SemaphoreType.DMA((len(sources),))],
        "first",
        *sources,
        space=pltpu.HBM,
    )
    fixed, lam = made[:7], made[7]
    id_a, id_b, hot, own_x, halo_x, v_own, m_own, xa, xb = made[8:]
    part_t = arr((2 * DOF, rows, lanes), f32)
    halo_tables = ()
    ids = (id_a, id_b)
    for step in range(ITERS):
        first, last = step == 0, step == ITERS - 1
        came_x = along_x(xa, xb)
        sent = message(GROUP * (2 if first else 1))
        own, ye, yo, part, halo = call(
            lambda *refs, first=first: window_kernel(first, False, *refs),
            (own_t, sent, sent, part_t, halo_t), work + table, "window",
            *fixed[:2], lam, *ids, hot, v_own, m_own, own_x,
        )
        came_y = along_y(*came_x, ye, yo)
        part = call(
            lambda *refs, first=first: side_kernel(first, *refs), part_t, table, "side",
            own_x, halo_x, v_own, m_own, *ids, part, *came_x, *halo_tables,
        )
        sent = message(LAST_GROUP if last else GROUP)
        outs = (lam_t, own_t, sent, sent) + (halo_t,) * (3 if first else 0 if last else 1)
        lam, own_x, xa, xb, *made = call(
            lambda *refs, first=first, last=last: middle_kernel(first, last, *refs), outs, table + work, "middle",
            *fixed, lam, *ids, hot, own_x, halo_x, own, halo, v_own, m_own, part, *came_x, *came_y, *halo_tables,
        )
        if not last:
            halo_x = made[0]
        if first:
            halo_tables = tuple(made[1:])
    came_x = along_x(xa, xb)
    own, ye, yo, lam = call(
        lambda *refs: window_kernel(False, True, *refs),
        (own_t, sent, sent, lam_t), work + table + [pltpu.SemaphoreType.DMA], "window",
        *fixed[:2], lam, *ids, hot, v_own, m_own, own_x,
        out_spaces=(pltpu.VMEM,) * 3 + (pltpu.HBM,),
    )
    came_y = along_y(*came_x, ye, yo)
    out = call(last_kernel, arr(start.shape, f32), [], "last", own_x, own, v_own, m_own, *came_x, *came_y)
    return lam.reshape(ROWS, 1, 1, rows, lanes), out.reshape(velocity0.shape)


def solution(mesh):
    whole = ("groups", "gx")
    body = P(None, whole, "gy", None)
    many = P(None, whole, "gy", None, None)
    one = P(whole, "gy", None, None)
    return jax.shard_map(
        on_device,
        mesh=mesh,
        in_specs=(body, body, many, many, many, many, one, many, one, one, one, one),
        out_specs=(many, body),
        check_vma=False,
    )
```

```python
import jax
import jax.numpy as jnp
import numpy as np
from jax import lax
from jax.experimental import pallas as pl
from jax.experimental.pallas import tpu as pltpu
from jax.sharding import PartitionSpec as P

ROWS = 3
DOF = 6
ITERS = 3
LANES = 128
NB = 2048
NBND = 256
CORNER = NBND // 8
OWN_TILES = NB // LANES
EDGE_TILES = 2
HALO_TILES = 9
CORNER_TILE = OWN_TILES - 1
HALO_CORNER = HALO_TILES - 1
SET_START = (0, 32, 288, 320, 576, 832, 864, 1120)
TABLE_START = (1920, 0, 1952, 256, 512, 1984, 768, 2016)
INTERIOR_START = 1152
INTERIOR_TABLE = 1024
EDGE_SLOTS = (1, 3, 4, 6)
CORNER_SLOTS = (0, 2, 5, 7)


def table_index(body):
    steps = []
    for slot in range(8):
        steps.append((SET_START[slot], TABLE_START[slot] - SET_START[slot]))
    steps.append((INTERIOR_START, INTERIOR_TABLE - INTERIOR_START))
    for slot in range(8):
        steps.append((NB + slot * NBND, TABLE_START[slot] - slot * NBND))
    shift = jnp.full(body.shape, steps[0][1], jnp.int32)
    for start, delta in steps[1:]:
        shift = jnp.where(body >= start, delta, shift)
    return body + shift


def lane_iota():
    return lax.broadcasted_iota(jnp.int32, (8, LANES), 1)


def to_tables(ref):
    zero = jnp.zeros((2, LANES), jnp.float32)
    blocks = [
        jnp.concatenate([ref[pl.ds(k, DOF, stride=OWN_TILES), :], zero], axis=0)
        for k in range(OWN_TILES)
    ]
    lane = lane_iota()
    tiles = []
    for slot in EDGE_SLOTS:
        first, off = divmod(SET_START[slot], LANES)
        rolled = [pltpu.roll(blocks[first + j], LANES - off, 1) for j in range(3)]
        for j in range(2):
            tiles.append(jnp.where(lane < LANES - off, rolled[j], rolled[j + 1]))
    tiles += blocks[INTERIOR_START // LANES :]
    corner = jnp.zeros((8, LANES), jnp.float32)
    for place, slot in enumerate(CORNER_SLOTS):
        block = blocks[SET_START[slot] // LANES]
        corner = jnp.where(lane // CORNER == place, block, corner)
    tiles.append(corner)
    return tiles


def from_tables(tiles, out_ref):
    lane = lane_iota()
    blocks = [jnp.zeros((8, LANES), jnp.float32) for _ in range(INTERIOR_START // LANES)]
    for e, slot in enumerate(EDGE_SLOTS):
        first, off = divmod(SET_START[slot], LANES)
        rolled = [pltpu.roll(tiles[2 * e + j], off, 1) for j in range(2)]
        blocks[first] = jnp.where(lane >= off, rolled[0], blocks[first])
        blocks[first + 1] = jnp.where(lane >= off, rolled[1], rolled[0])
        blocks[first + 2] = jnp.where(lane < off, rolled[1], blocks[first + 2])
    for place, slot in enumerate(CORNER_SLOTS):
        k = SET_START[slot] // LANES
        blocks[k] = jnp.where(lane // CORNER == place, tiles[CORNER_TILE], blocks[k])
    blocks += tiles[8:CORNER_TILE]
    for k in range(OWN_TILES):
        out_ref[pl.ds(k, DOF, stride=OWN_TILES), :] = blocks[k][:DOF]


def row_of(ref, r):
    return ref[pl.ds(r, 1), :]


def build_onehot(index, onehot_ref):
    rows = index.shape[0]
    lane = (index & (NBND - 1)).astype(jnp.float32).T
    base = lax.broadcasted_iota(jnp.int32, (LANES, NBND), 1).astype(jnp.float32).astype(jnp.bfloat16)
    one, zero = jnp.ones((), jnp.bfloat16), jnp.zeros((), jnp.bfloat16)
    for r in range(rows):
        q = jnp.broadcast_to(lane[:, r : r + 1], (LANES, LANES)).astype(jnp.bfloat16)
        q = jnp.concatenate([q, q], axis=1)
        onehot_ref[r * LANES : (r + 1) * LANES, :] = jnp.where(base == q, one, zero)


def forces(lam, jac_ref, force_ref):
    rows = lam[0].shape[0]
    for d in range(DOF):
        f = jac_ref[d] * lam[0]
        f = f + jac_ref[DOF + d] * lam[1]
        f = f + jac_ref[2 * DOF + d] * lam[2]
        force_ref[d * rows : (d + 1) * rows, :] = f
    for d in range(DOF, 8):
        force_ref[d * rows : (d + 1) * rows, :] = jnp.zeros_like(f)


def spread(force_ref, index_ref, left_ref, heads):
    rows = index_ref.shape[0]
    for r in range(rows):
        f = force_ref[pl.ds(r, 8, stride=rows), :]
        hi = f.astype(jnp.bfloat16).astype(jnp.float32)
        lo = f - hi
        head = jnp.broadcast_to(row_of(index_ref, r) >> 8, (8, LANES))
        for k, h in enumerate(heads):
            mask = head == h
            both = jnp.concatenate([jnp.where(mask, hi, 0.0), jnp.where(mask, lo, 0.0)], axis=0)
            left_ref[16 * k : 16 * (k + 1), r * LANES : (r + 1) * LANES] = both.astype(jnp.bfloat16)


X_HEADS = (0, 3, 7)
REST_HEADS = (1, 2, 4, 5, 6)


def with_halo(heads):
    return heads + tuple(h + 8 for h in heads if h < 4 or h == 7)


def scatter(lam, jac_a, jac_b, id_a, id_b, hot, force, left, heads, between=None):
    contacts = hot.shape[0] // 2
    both = with_halo(heads)
    rows, own_rows = 16 * len(both), 16 * len(heads)
    forces(lam, jac_a, force)
    spread(force, id_a, left.at[:own_rows, :contacts], heads)
    left[own_rows:rows, :contacts] = jnp.zeros((rows - own_rows, contacts), jnp.bfloat16)
    if between is not None:
        sums = jnp.dot(left[:rows, :contacts], hot[:contacts, :], preferred_element_type=jnp.float32)
        between()
    forces(lam, jac_b, force)
    spread(force, id_b, left.at[:rows, contacts:], both)
    if between is None:
        sums = jnp.dot(left[:rows, :], hot[...], preferred_element_type=jnp.float32)
    else:
        sums = sums + jnp.dot(left[:rows, contacts:], hot[contacts:, :], preferred_element_type=jnp.float32)

    def tile(k, j):
        lanes = slice(j * LANES, (j + 1) * LANES)
        return sums[16 * k : 16 * k + 8, lanes] + sums[16 * k + 8 : 16 * k + 16, lanes]

    own, halo = {}, {}
    for k, h in enumerate(both):
        for j in range(2):
            if h < 8:
                own[2 * h + j] = tile(k, j)
            elif h < 12:
                halo[2 * (h - 8) + j] = tile(k, j)
    if 15 in both:
        halo[HALO_CORNER] = tile(both.index(15), 1)
    return own, halo


def is_even():
    return lax.rem(lax.axis_index("gy"), 2) == 0


GROUP = 32
LAST_GROUP = 24


def put_edges(even, group, minus, plus, a_ref, b_ref):
    for k, (m, p) in enumerate(zip(minus, plus)):
        rows = slice(group + DOF * k, group + DOF * (k + 1))
        a_ref[rows, :] = jnp.where(even, m[:DOF], p[:DOF])
        b_ref[rows, :] = jnp.where(even, p[:DOF], m[:DOF])


def blocks(tiles):
    block = lane_iota() // CORNER
    out = tiles[3]
    for k in range(3):
        out = jnp.where(block == k, tiles[k], out)
    return out


def put_x(even, groups, a_ref, b_ref):
    size = a_ref.shape[0] // len(groups)
    for g, (first, second) in enumerate(groups):
        up, down = [second[6], second[7]], [second[0], second[1]]
        if first is not None:
            up, down = [first[6], first[7]] + up, [first[0], first[1]] + down
        theirs = second[CORNER_TILE] if CORNER_TILE in second else second[HALO_CORNER]
        ours = jnp.zeros_like(theirs) if first is None else first[CORNER_TILE]
        ours_on, theirs_on = pltpu.roll(ours, CORNER, 1), pltpu.roll(theirs, CORNER, 1)
        theirs_half = pltpu.roll(theirs, 2 * CORNER, 1)
        corner_down = blocks([ours, theirs_on, ours_on, theirs_half])
        corner_up = blocks([ours_on, theirs_half, ours, theirs_on])
        put_edges(even, g * size, down, up, a_ref, b_ref)
        last = slice((g + 1) * size - 8, (g + 1) * size)
        a_ref[last, :] = jnp.where(even, corner_down, corner_up)
        b_ref[last, :] = jnp.where(even, corner_up, corner_down)


class Received:
    def __init__(self, even, a_ref, b_ref, e_ref=None, o_ref=None):
        def pick(when, other):
            def tile(row):
                return jnp.where(even, when[pl.ds(row, 8), :], other[pl.ds(row, 8), :])

            return tile

        self.rows = GROUP if a_ref.shape[0] % GROUP == 0 else LAST_GROUP
        self.x_low, self.x_high = pick(b_ref, a_ref), pick(a_ref, b_ref)
        if e_ref is not None:
            self.y_low, self.y_high = pick(e_ref, o_ref), pick(o_ref, e_ref)

    def edge(self, side, plane):
        place = 2 * (plane % 2) if self.rows == GROUP else 0
        base = self.rows * (plane // 2) + DOF * place
        return [side(base), side(base + DOF)]

    def corner(self, plane):
        odd = (lane_iota() & CORNER) != 0
        row = self.rows * (plane // 2) + self.rows - 8
        low, high = self.y_low(row), self.y_high(row)
        if plane % 2:
            return jnp.where(odd, pltpu.roll(high, 2 * CORNER, 1), pltpu.roll(low, 3 * CORNER, 1))
        return jnp.where(odd, pltpu.roll(high, 3 * CORNER, 1), low)


X_EDGES = (0, 1, 6, 7)
Y_EDGES = (2, 3, 4, 5)
INTERIOR = tuple(range(8, CORNER_TILE))


def x_plane(came, plane):
    low, high = came.edge(came.x_low, plane), came.edge(came.x_high, plane)
    return dict(zip(X_EDGES, low + high))


def y_plane(came, plane):
    low, high = came.edge(came.y_low, plane), came.edge(came.y_high, plane)
    return dict(zip(Y_EDGES, low + high))


def put_dict(ref, tiles):
    for t, value in tiles.items():
        ref[t] = value


def first_kernel(*refs):
    sources, kept, outs = refs[:12], refs[12:20], refs[20:29]
    body_a, body_b, start, minv, force, left, sems = refs[29:]
    id_a, id_b, hot, own, halo, v_own, m_own, xa, xb = outs
    jac_a, jac_b, precond, bias, mu, stick, act, lam0 = kept
    goals = (body_a, body_b, act, lam0, jac_a, jac_b, start, minv, precond, bias, mu, stick)
    copies = [pltpu.make_async_copy(s, g, sems.at[k]) for k, (s, g) in enumerate(zip(sources, goals))]
    for copy in copies:
        copy.start()
    even = is_even()
    copies[0].wait()
    id_a[...] = table_index(body_a[...])
    build_onehot(id_a[...], hot.at[: hot.shape[0] // 2])
    copies[1].wait()
    id_b[...] = table_index(body_b[...])
    for copy in copies[2:6]:
        copy.wait()
    active = act[...].astype(jnp.float32)
    lam = [active * lam0[k] for k in range(ROWS)]
    for k in range(ROWS):
        lam0[k] = lam[k]
    v, m = [], []

    def between():
        build_onehot(id_b[...], hot.at[hot.shape[0] // 2 :])
        v.extend(to_tables(start))
        m.extend(to_tables(minv))
        for t in range(OWN_TILES):
            v_own[t], m_own[t] = v[t], m[t]

    for copy in copies[6:8]:
        copy.wait()
    sums, sums_halo = scatter(lam, jac_a, jac_b, id_a, id_b, hot, force, left, X_HEADS, between)
    put_dict(own, sums)
    put_dict(halo, sums_halo)
    put_x(even, [(sums, sums_halo), (dict(enumerate(v)), dict(enumerate(m)))], xa, xb)
    for copy in copies[8:]:
        copy.wait()


def turn_kernel(ra, rb, e_in, o_in, e_ref, o_ref):
    even = is_even()
    came = Received(even, ra, rb)
    left = lane_iota() < 2 * CORNER
    for g in range(0, ra.shape[0], came.rows):
        row = g + came.rows - 8
        low, high = came.x_low(row), came.x_high(row)
        minus, plus = jnp.where(left, high, low), jnp.where(left, low, high)
        e_ref[row : row + 8, :] = jnp.where(even, minus, plus)
        o_ref[row : row + 8, :] = jnp.where(even, plus, minus)


def gather(table, index, codes, start=None):
    values = [[] for _ in range(DOF)]
    for g in range(0, index.shape[0], 8):
        lane = index[g : g + 8] & (LANES - 1)
        code = index[g : g + 8] >> 7
        if start is None:
            part = [jnp.zeros(lane.shape, jnp.float32) for _ in range(DOF)]
        else:
            part = [start[d, g : g + 8, :] for d in range(DOF)]
        for c, t in codes:
            mask = code == c
            for d in range(DOF):
                row = jnp.broadcast_to(table[t, d : d + 1, :], lane.shape)
                got = jnp.take_along_axis(row, lane, axis=1, mode="promise_in_bounds")
                part[d] = jnp.where(mask, got, part[d])
        for d in range(DOF):
            values[d].append(part[d])
    return [jnp.concatenate(v, axis=0) for v in values]


def own_codes(tiles):
    return tuple((t, t) for t in tiles)


def halo_codes(tiles):
    return tuple((OWN_TILES + (15 if t == HALO_CORNER else t), OWN_TILES + t) for t in tiles)


def gather_both(table, id_a, id_b, own_tiles, halo_tiles, out, start):
    part = (None, None) if start is None else (start.at[:DOF], start.at[DOF:])
    for ref, ids, codes, first, base in (
        (out, id_a, own_codes(own_tiles), part[0], 0),
        (out, id_b, own_codes(own_tiles) + halo_codes(halo_tiles), part[1], DOF),
    ):
        for d, value in enumerate(gather(table, ids[...], codes, first)):
            ref[base + d] = value


def window_kernel(first, last, jac_a, jac_b, lam, id_a, id_b, hot, v_own, m_own, own_x, *refs):
    own, e_ref, o_ref, out = refs[:4]
    halo, work = (None, refs[4:]) if last else (refs[4], refs[5:])
    force, left, table, *sem = work
    if last:
        copy = pltpu.make_async_copy(lam, out, sem[0])
        copy.start()
    even = is_even()
    values = [lam[k] for k in range(ROWS)]
    sums, sums_halo = scatter(values, jac_a, jac_b, id_a, id_b, hot, force, left, REST_HEADS)
    put_dict(own, sums)
    if not last:
        put_dict(halo, sums_halo)
    planes = [(sums_halo,)] if last else [(sums, sums_halo)] + [(v_own, m_own)] * first
    size = e_ref.shape[0] // len(planes)
    for g, pair in enumerate(planes):
        minus = [p[t] for p in pair for t in (2, 3)]
        plus = [p[t] for p in pair for t in (4, 5)]
        put_edges(even, g * size, minus, plus, e_ref, o_ref)
    if last:
        copy.wait()
        return
    for t in INTERIOR:
        table[t] = v_own[t] + m_own[t] * (sums[t] if t in sums else own_x[t])
    gather_both(table, id_a, id_b, INTERIOR, (), out, None)


def side_kernel(first, own, halo, v_own, m_own, id_a, id_b, part, ra, rb, *refs):
    v_halo, m_halo, (out, table) = (None, None, refs) if first else (refs[0], refs[1], refs[2:])
    came = Received(is_even(), ra, rb)
    theirs, ours = x_plane(came, 0), x_plane(came, 1)
    if first:
        v_halo, m_halo = x_plane(came, 2), x_plane(came, 3)
    for t in X_EDGES:
        table[t] = v_own[t] + m_own[t] * (own[t] + ours[t])
        table[OWN_TILES + t] = v_halo[t] + m_halo[t] * (halo[t] + theirs[t])
    gather_both(table, id_a, id_b, X_EDGES, X_EDGES, out, part)


def relative(jac, values):
    out = []
    for k in range(ROWS):
        u = jac[k * DOF] * values[0]
        for d in range(1, DOF):
            u = u + jac[k * DOF + d] * values[d]
        out.append(u)
    return out


def middle_kernel(
    first, last, jac_a, jac_b, precond, bias, mu, stick, act, lam_in,
    id_a, id_b, hot, own_x, halo_x, own, halo, v_own, m_own, part, ra, rb, qe, qo, *refs,
):
    if not first:
        v_halo, m_halo, *refs = refs
    lam_out, own_out, xa, xb, *made = refs[:-3]
    table, force, left = refs[-3:]
    if first:
        v_halo, m_halo = made[1:]
    even = is_even()
    came = Received(even, ra, rb, qe, qo)
    if first:
        for ref, p in ((v_halo, 2), (m_halo, 3)):
            for t, value in (x_plane(came, p) | y_plane(came, p)).items():
                ref[t] = value
            ref[HALO_CORNER] = came.corner(p)
    theirs, ours = y_plane(came, 0), y_plane(came, 1)
    theirs[HALO_CORNER], ours[CORNER_TILE] = came.corner(0), came.corner(1)
    for t, value in ours.items():
        mine = own_x if t == CORNER_TILE else own
        table[t] = v_own[t] + m_own[t] * (mine[t] + value)
    for t, value in theirs.items():
        mine = halo_x if t == HALO_CORNER else halo
        table[OWN_TILES + t] = v_halo[t] + m_halo[t] * (mine[t] + value)
    late, late_halo = own_codes(ours), halo_codes(theirs)
    v_a = gather(table, id_a[...], late, part.at[:DOF])
    v_b = gather(table, id_b[...], late + late_halo, part.at[DOF:])
    u_a = relative(jac_a, v_a)
    u_b = relative(jac_b, v_b)
    target = [u_a[k] + u_b[k] + bias[k] for k in range(ROWS)]
    active = act[...].astype(jnp.float32)
    lam = [lam_in[k] for k in range(ROWS)]
    raw = []
    for k in range(ROWS):
        w = precond[k * ROWS] * target[0]
        for j in range(1, ROWS):
            w = w + precond[k * ROWS + j] * target[j]
        raw.append(lam[k] - w)
    normal = jnp.maximum(raw[0], 0.0)
    bound = mu[...] * (1.0 + 0.5 * stick[...].astype(jnp.float32)) * normal + 0.1
    square = raw[1] * raw[1] + raw[2] * raw[2]
    scale = bound / jnp.sqrt(jnp.maximum(square, bound * bound))
    lam = [active * normal, active * (raw[1] * scale), active * (raw[2] * scale)]
    for k in range(ROWS):
        lam_out[k] = lam[k]
    sums, sums_halo = scatter(lam, jac_a, jac_b, id_a, id_b, hot, force, left, X_HEADS)
    put_dict(own_out, sums)
    if not last:
        put_dict(made[0], sums_halo)
    put_x(even, [(None if last else sums, sums_halo)], xa, xb)


def last_kernel(own_x, own, v_own, m_own, ra, rb, qe, qo, out):
    came = Received(is_even(), ra, rb, qe, qo)
    ours = x_plane(came, 1) | y_plane(came, 1)
    ours[CORNER_TILE] = came.corner(1)
    mine = [(own_x if t // 2 in X_HEADS else own)[t] for t in range(OWN_TILES)]
    total = [mine[t] + ours[t] if t in ours else mine[t] for t in range(OWN_TILES)]
    from_tables([v_own[t] + m_own[t] * total[t] for t in range(OWN_TILES)], out)


def exchange_pairs(nx, ny):
    up = []
    for x in range(nx):
        for y in range(ny):
            to = x + 1 if y % 2 == 1 else x - 1
            goal = (to, y) if 0 <= to < nx else (x, y ^ 1)
            up.append((x * ny + y, goal[0] * ny + goal[1]))
    down = [(b, a) for a, b in up]
    near = [(y, y ^ 1) for y in range(ny)]
    far = [(y, (((y + 1) ^ 1) - 1) % ny) for y in range(ny)]
    return up, down, near, far


def on_device(
    velocity0, inv_mass, jac_a, jac_b, precond, bias, friction, impulse0, body_a, body_b, active, sticking
):
    nx, ny = lax.axis_size("gx"), lax.axis_size("gy")
    up, down, near, far = exchange_pairs(nx, ny)
    rows, lanes = body_a.shape[-2:]
    flat = lambda a: a.reshape(-1, rows, lanes)
    plain = lambda a: a.reshape(rows, lanes)
    jac_a, jac_b, precond, bias, impulse0 = map(flat, (jac_a, jac_b, precond, bias, impulse0))
    friction, body_a, body_b, active, sticking = map(plain, (friction, body_a, body_b, active, sticking))
    start, minv = (a.reshape(-1, lanes) for a in (velocity0, inv_mass))
    contacts = rows * lanes
    f32, i32, bf16 = jnp.float32, jnp.int32, jnp.bfloat16
    arr = jax.ShapeDtypeStruct
    vmem = pl.BlockSpec(memory_space=pltpu.VMEM)
    own_t, halo_t = arr((OWN_TILES, 8, lanes), f32), arr((HALO_TILES, 8, lanes), f32)
    lam_t = arr((ROWS, rows, lanes), f32)
    ids_t, hot_t = arr((rows, lanes), i32), arr((2 * contacts, NBND), bf16)
    message = lambda r: arr((r, lanes), f32)
    work = [
        pltpu.VMEM((8 * rows, lanes), f32),
        pltpu.VMEM((16 * len(with_halo(REST_HEADS)), 2 * contacts), bf16),
    ]
    table = [pltpu.VMEM((OWN_TILES + HALO_TILES, 8, lanes), f32)]

    def call(kernel, outs, scratch, name, *operands, space=pltpu.VMEM, out_spaces=None, aliases={}, flops=0):
        spaces = out_spaces or jax.tree.map(lambda _: pltpu.VMEM, outs)
        return pl.pallas_call(
            kernel,
            out_shape=outs,
            in_specs=[pl.BlockSpec(memory_space=space)] * len(operands),
            out_specs=jax.tree.map(lambda m: pl.BlockSpec(memory_space=m), spaces),
            scratch_shapes=scratch,
            input_output_aliases=aliases,
            compiler_params=pltpu.CompilerParams(vmem_limit_bytes=32 * 1024 * 1024),
            cost_estimate=pl.CostEstimate(flops=flops, bytes_accessed=0, transcendentals=0) if flops else None,
            name=name,
        )(*operands)

    def along_x(xa, xb):
        return lax.ppermute(xa, ("gx", "gy"), up), lax.ppermute(xb, ("gx", "gy"), down)

    def along_y(ra, rb, ye, yo):
        like = arr(ye.shape, f32)
        ye, yo = call(turn_kernel, (like, like), [], "turn", ra, rb, ye, yo, aliases={2: 0, 3: 1})
        return lax.ppermute(ye, "gy", far), lax.ppermute(yo, "gy", near)

    sources = (body_a, body_b, active, impulse0, jac_a, jac_b, start, minv, precond, bias, friction, sticking)
    like = lambda a: arr(a.shape, a.dtype)
    kept = (jac_a, jac_b, precond, bias, friction, sticking, active, impulse0)
    sources = [pltpu.with_memory_space_constraint(a, pltpu.HBM) for a in sources]
    made = call(
        first_kernel,
        (*map(like, kept), ids_t, ids_t, hot_t, own_t, halo_t, own_t, own_t, message(2 * GROUP), message(2 * GROUP)),
        [pltpu.VMEM(a.shape, a.dtype) for a in (body_a, body_b, start, minv)]
        + work
        + [pltpu.SemaphoreType.DMA((len(sources),))],
        "first",
        *sources,
        space=pltpu.HBM,
    )
    fixed, lam = made[:7], made[7]
    id_a, id_b, hot, own_x, halo_x, v_own, m_own, xa, xb = made[8:]
    part_t = arr((2 * DOF, rows, lanes), f32)
    halo_tables = ()
    ids = (id_a, id_b)
    for step in range(ITERS):
        first, last = step == 0, step == ITERS - 1
        came_x = along_x(xa, xb)
        sent = message(GROUP * (2 if first else 1))
        own, ye, yo, part, halo = call(
            lambda *refs, first=first: window_kernel(first, False, *refs),
            (own_t, sent, sent, part_t, halo_t), work + table, "window",
            *fixed[:2], lam, *ids, hot, v_own, m_own, own_x,
        )
        came_y = along_y(*came_x, ye, yo)
        part = call(
            lambda *refs, first=first: side_kernel(first, *refs), part_t, table, "side",
            own_x, halo_x, v_own, m_own, *ids, part, *came_x, *halo_tables,
        )
        sent = message(LAST_GROUP if last else GROUP)
        outs = (lam_t, own_t, sent, sent) + (halo_t,) * (3 if first else 0 if last else 1)
        lam, own_x, xa, xb, *made = call(
            lambda *refs, first=first, last=last: middle_kernel(first, last, *refs), outs, table + work, "middle",
            *fixed, lam, *ids, hot, own_x, halo_x, own, halo, v_own, m_own, part, *came_x, *came_y, *halo_tables,
        )
        if not last:
            halo_x = made[0]
        if first:
            halo_tables = tuple(made[1:])
    came_x = along_x(xa, xb)
    own, ye, yo, lam = call(
        lambda *refs: window_kernel(False, True, *refs),
        (own_t, sent, sent, lam_t), work + table + [pltpu.SemaphoreType.DMA], "window",
        *fixed[:2], lam, *ids, hot, v_own, m_own, own_x,
        out_spaces=(pltpu.VMEM,) * 3 + (pltpu.HBM,),
    )
    came_y = along_y(*came_x, ye, yo)
    out = call(last_kernel, arr(start.shape, f32), [], "last", own_x, own, v_own, m_own, *came_x, *came_y)
    return lam.reshape(ROWS, 1, 1, rows, lanes), out.reshape(velocity0.shape)


def solution(mesh):
    whole = ("groups", "gx")
    body = P(None, whole, "gy", None)
    many = P(None, whole, "gy", None, None)
    one = P(whole, "gy", None, None)
    return jax.shard_map(
        on_device,
        mesh=mesh,
        in_specs=(body, body, many, many, many, many, one, many, one, one, one, one),
        out_specs=(many, body),
        check_vma=False,
    )
```
